256 devices in a mesh: group: 2 (over core), dp: 16 (over x, y), head: 8 (over z).
Axes of the slice: x: 4, y: 4, z: 8, core: 2. Of those that a mesh axis runs over, the one named last changes fastest.
Arguments:
- queries: bfloat16 [2, 512, 64, 576], P('group', 'dp', 'head'), may hold values from -400 to 400
- latent_cache: bfloat16 [2, 512, 192, 576], P('group', 'dp'), may hold values from -9 to 9
- lengths: int32 [2, 512], P('group', 'dp'), may hold values from 2 to 192, as said below
- w_value: bfloat16 [64, 512, 128], P('head'), may hold values from -0.25 to 0.25
- w_out: bfloat16 [8192, 7168], P('head', 'dp'), may hold values from -0.0625 to 0.0625
- residual: bfloat16 [2, 512, 7168], P('group', ('dp', 'head')), may hold values from -6 to 6
- norm_gain: float32 [7168], replicated, may hold values from 0.5 to 1.5
- routes: int32 [2, 512, 8], P('group', ('dp', 'head')), may hold values from 0 to 15, all different within a row; in each aligned block of 4 rows (0 to 3, 4 to 7, ..., all dimensions but the last counted through in order) at most 3 rows name the same one
- gate_weights: float32 [2, 512, 8], P('group', ('dp', 'head')), may hold values from 0.2 to 1
- w_gate: bfloat16 [16, 7168, 2048], P('dp', None, ('group', 'head')), may hold values from -0.0625 to 0.0625
- w_up: bfloat16 [16, 7168, 2048], P('dp', None, ('group', 'head')), may hold values from -0.0625 to 0.0625
- w_down: bfloat16 [16, 7168, 2048], P('dp', None, ('group', 'head')), may hold values from -0.125 to 0.125
Outputs:
- layer_out: bfloat16 [2, 512, 7168], P('group', ('dp', 'head'))
The draws below stay inside these ranges and needn't reach their ends.
Inputs may be any that keep to these rules, and one draw needn't show every extreme that they name: `lengths`: some request has exactly 192 cached tokens. `routes`: the 8 experts of a token differ; among the 4 rows of one device (aligned blocks along the requests of both micro-batches in order) no expert is named by more than 3 rows, and that bound is reached.
All inputs are finite; a program needn't handle non-finite values.
Results may differ from the reference program's by a relative error of at most 0.029.
Values may be sent and summed in bfloat16 or wider, within the bound.
No kernel may reach another device: no remote copies, remote signals or barrier semaphores. Data moves between devices by JAX's collectives and lax.ppermute only.
A program may use at most 128 MiB of HBM per device.

```python
import math
import jax
import jax.numpy as jnp
import numpy as np
from jax import lax

D = 7168
FFH = 2048
H = 64
LAT = 512
ROPE = 64
VHEAD = 128
EXPERTS = 16
TOP = 8
ROWS = 4
LEN = 192
CAP = 3
REQS = 512
N_GROUP = 2


def shared_latents(key):
    return 1.5 * jax.random.normal(key, (N_GROUP, REQS, LEN, LAT + ROPE), jnp.float32)


def draw_latent_cache(key, part):
    latents = shared_latents(key)
    return jnp.clip(latents, -9.0, 9.0).astype(jnp.bfloat16)


def draw_queries(key, part):
    key = jax.random.fold_in(key, 5)
    query = jax.random.normal(key, (N_GROUP, REQS, H, LAT + ROPE), jnp.float32)
    return query.astype(jnp.bfloat16)


def draw_lengths(key, part):
    key = jax.random.fold_in(key, 7)
    drawn = jax.random.randint(key, (N_GROUP, REQS), 2, LEN + 1)
    return drawn.at[0, 0].set(LEN).astype(jnp.int32)


def block_scale(rng, shape, pieces, least, largest):
    def one(axis_at, shards_of):
        steps = jax.random.uniform(jax.random.fold_in(jax.random.fold_in(rng, 6), axis_at), (shards_of,), jnp.float32, least / len(pieces), largest / len(pieces))
        return jnp.repeat(jnp.exp(steps), shape[axis_at] // shards_of).reshape((-1,) + (1,) * (len(shape) - axis_at - 1))

    gain = one(*pieces[0])
    for cut in pieces[1:]:
        gain = gain * one(*cut)
    return gain


def deal_out(own_key, own, number, rows, amount, top, bound, skew):
    ranking = jax.random.permutation(own_key, amount)
    crowded, common = portions_of(amount, rows * top, bound, skew, True), portions_of(amount, rows * top, bound, skew, False)
    places = jnp.arange(amount)

    def named(tallies, turn):
        used = int((tallies > 0).sum())
        fixed = max(1, used // 4)
        passed = fixed + (places - fixed + turn * (used - fixed)) % max(1, amount - fixed)
        return jnp.zeros((amount,), jnp.int32).at[ranking[jnp.where(places < fixed, places, passed)]].set(jnp.asarray(tallies, jnp.int32))

    tallies = jnp.where(number % 4 == 0, named(crowded, number // 4), named(common, number - number // 4 - 1))
    mixed = jax.random.permutation(jax.random.fold_in(own, 3), amount)
    source_of, taker = mixed[0:amount // 2 * 2:2], mixed[1:amount // 2 * 2:2]
    slack = jnp.minimum(tallies[source_of] - 1, bound - tallies[taker]) // 2
    slack = jnp.where((source_of == ranking[0]) | (taker == ranking[0]) | (tallies[taker] == 0), 0, jnp.maximum(slack, 0))
    passed = jax.random.randint(jax.random.fold_in(own, 4), (amount // 2,), 0, 1 << 20) % (slack + 1)
    tallies = tallies.at[source_of].add(-passed).at[taker].add(passed)
    members = jnp.searchsorted(jnp.cumsum(tallies), jnp.arange(rows * top), side="right").astype(jnp.int32)
    listing = members.reshape(top, rows).T
    listing = listing[jax.random.permutation(jax.random.fold_in(own, 1), rows)]
    turn = jax.random.randint(jax.random.fold_in(own, 2), (rows, 1), 0, top)
    return jnp.take_along_axis(listing, (jnp.arange(top)[None, :] + turn) % top, axis=1)


def portions_of(number_of, total, most, skew, full):
    portions = [(1 << 20) // math.isqrt(grade ** skew) + 1 for grade in range(1, number_of + 1)]
    largest = most if full else min(most, max(-(-total // number_of), total * portions[0] // sum(portions)))
    least = 1 if total - largest >= number_of - 1 else 0
    given, spare = [largest] + [least] * (number_of - 1), total - largest - least * (number_of - 1)
    while spare > 0:
        free = [i for i in range(1, number_of) if given[i] < largest] or [i for i in range(1, number_of) if given[i] < most]
        pool, remaining = sum([portions[i] for i in free]), spare
        for i in free:
            extra = min(most - given[i], max(1, remaining * portions[i] // pool), spare)
            given[i] = given[i] + extra
            spare = spare - extra
    return np.array(given)


def scatter_about(rng, extent, width, bound, shards=(), kind=jnp.bfloat16):
    array = jax.random.normal(rng, extent, jnp.float32) * width
    if len(shards) > 0:
        array = block_scale(rng, extent, shards, -0.22, 0.18) * array
    return jnp.clip(array, min=-bound, max=bound).astype(kind)


def setup_inputs(seed: int = 0) -> dict:
    splits = jax.random.split(jax.random.key(seed), 13)
    queries = draw_queries(jax.random.fold_in(splits[12], 71), 0)
    latent_cache = draw_latent_cache(jax.random.fold_in(splits[12], 71), 0)
    lengths = draw_lengths(jax.random.fold_in(splits[12], 71), 0)
    w_value = scatter_about(splits[3], (H, LAT, VHEAD), LAT ** -0.5, 0.25, ((0, 8),))
    w_out = scatter_about(splits[4], (H * VHEAD, D), (H * VHEAD) ** -0.5, 0.0625, ((0, 8), (1, 16)))
    residual = scatter_about(splits[5], (N_GROUP, REQS, D), 1.0, 6.0, ((0, 2), (1, 128)))
    norm_gain = jnp.clip(1.0 + 0.1 * jax.random.normal(splits[6], (D,), jnp.float32), 0.5, 1.5)
    routes_keys = jax.random.split(jax.random.fold_in(splits[7], 1), N_GROUP * REQS // ROWS)
    routes_turns = jax.random.permutation(jax.random.fold_in(splits[7], 3), N_GROUP * REQS // ROWS)
    routes = jax.vmap(lambda own, number: deal_out(jax.random.fold_in(splits[7], 2), own, number, ROWS, EXPERTS, TOP, CAP, 2))(routes_keys, routes_turns).reshape((N_GROUP, REQS, TOP))
    gate_weights = jnp.clip(jnp.exp(math.log(1.0) - 1.609438 * jax.random.uniform(splits[8], (N_GROUP, REQS, TOP), jnp.float32) ** block_scale(splits[8], (N_GROUP, REQS, TOP), ((0, 2), (1, 128)), -0.2, 0.2)), 0.2, 1.0)
    w_gate = scatter_about(splits[9], (EXPERTS, D, FFH), D ** -0.5, 0.0625, ((0, 16), (2, 16)))
    w_up = scatter_about(splits[10], (EXPERTS, D, FFH), D ** -0.5, 0.0625, ((0, 16), (2, 16)))
    w_down = scatter_about(splits[11], (EXPERTS, D, FFH), FFH ** -0.5, 0.125, ((0, 16), (2, 16)))
    return {"queries": queries, "latent_cache": latent_cache, "lengths": lengths, "w_value": w_value, "w_out": w_out, "residual": residual, "norm_gain": norm_gain, "routes": routes, "gate_weights": gate_weights, "w_gate": w_gate, "w_up": w_up, "w_down": w_down}


softmax_scale = 0.07216878364870323
norm_eps = 1e-06

def attend_request(operands):
    query, cached, length = operands
    query_f = query.astype(jnp.float32)
    keys = cached.astype(jnp.float32)
    scores = jnp.dot(query_f, keys.T, preferred_element_type=jnp.float32) * softmax_scale
    visible = jnp.arange(keys.shape[0], dtype=jnp.int32) < length
    scores = jnp.where(visible[None, :], scores, -jnp.inf)
    row_max = lax.optimization_barrier(jnp.max(scores, axis=1, keepdims=True))
    weights = jnp.exp(scores - row_max)
    shares = (weights / lax.optimization_barrier(jnp.sum(weights, axis=1, keepdims=True))).astype(jnp.bfloat16)
    latent = jnp.dot(shares.astype(jnp.float32), keys[:, :LAT], preferred_element_type=jnp.float32)
    return latent.astype(jnp.bfloat16)

def reference(queries, latent_cache, lengths, w_value, w_out, residual, norm_gain, routes, gate_weights, w_gate, w_up, w_down):
    groups, requests, heads_all, feature_width = queries.shape
    flattened = (queries.reshape(groups * requests, heads_all, feature_width), latent_cache.reshape(groups * requests, latent_cache.shape[2], feature_width), lengths.reshape(-1))
    latents = lax.map(attend_request, flattened)
    head_values = jnp.einsum('rhc,hcv->rhv', latents.astype(jnp.float32), w_value.astype(jnp.float32)).astype(jnp.bfloat16)
    concat = head_values.reshape(groups * requests, heads_all * w_value.shape[2])
    attended = jnp.dot(concat, w_out, preferred_element_type=jnp.float32).astype(jnp.bfloat16)
    hidden = (residual.reshape(groups * requests, -1).astype(jnp.float32) + attended.astype(jnp.float32)).astype(jnp.bfloat16)
    hidden_f = hidden.astype(jnp.float32)
    mean_square = lax.optimization_barrier(jnp.mean(hidden_f * hidden_f, axis=1, keepdims=True))
    normed = (hidden_f * lax.rsqrt(mean_square + norm_eps) * norm_gain).astype(jnp.bfloat16)
    expert_ids = jnp.arange(EXPERTS, dtype=jnp.int32)
    chosen = (routes.reshape(-1, TOP)[:, :, None] == expert_ids[None, None, :]).astype(jnp.float32)
    table = lax.optimization_barrier(jnp.sum(gate_weights.reshape(-1, TOP)[:, :, None] * chosen, axis=1))
    normed_f = normed.astype(jnp.float32)

    def one_expert(running, operands):
        gate_w, up_w, down_w, column = operands
        gate = jnp.dot(normed_f, gate_w.astype(jnp.float32), preferred_element_type=jnp.float32)
        upward = jnp.dot(normed_f, up_w.astype(jnp.float32), preferred_element_type=jnp.float32)
        active = (jax.nn.silu(gate) * upward).astype(jnp.bfloat16)
        result = jnp.dot(active.astype(jnp.float32), down_w.astype(jnp.float32).T, preferred_element_type=jnp.float32).astype(jnp.bfloat16)
        return (running + column[:, None] * result.astype(jnp.float32), 0)
    mixture, unused = lax.scan(one_expert, jnp.zeros(hidden.shape, jnp.float32), (w_gate, w_up, w_down, table.T))
    layer_out = (hidden_f + mixture).astype(jnp.bfloat16)
    return layer_out.reshape(residual.shape)
```

```python
import jax
import jax.numpy as jnp
from jax import lax
from jax.sharding import PartitionSpec as P

EXPERTS = 16
CAP = 3


softmax_scale = 0.07216878364870323
norm_eps = 1e-06
bf16 = jnp.bfloat16
f32 = jnp.float32


def local(
    queries,
    latent_cache,
    lengths,
    w_value,
    w_out,
    residual,
    norm_gain,
    routes,
    gate_weights,
    w_gate,
    w_up,
    w_down,
):
    reqs = queries.shape[1]
    heads = queries.shape[2]
    latent_width = w_value.shape[1]
    value_width = w_value.shape[2]
    span = latent_cache.shape[2]
    rows = residual.shape[1]
    width = residual.shape[2]
    n_group = lax.axis_size("group")
    n_dp = lax.axis_size("dp")
    n_head = lax.axis_size("head")
    n_col = n_group * n_head
    cols = width // n_dp
    piece = width // n_col
    g = lax.axis_index("group")
    dp = lax.axis_index("dp")
    z = lax.axis_index("head")

    down = lax.all_to_all(
        w_down[0].reshape(n_col, piece, w_down.shape[2]),
        ("group", "head"),
        split_axis=0,
        concat_axis=0,
        tiled=True,
    )

    expert_ids = jnp.arange(EXPERTS, dtype=jnp.int32)
    chosen = routes[0][:, :, None] == expert_ids[None, None, :]
    table = jnp.max(jnp.where(chosen, gate_weights[0][:, :, None], -1.0), axis=1)
    table = lax.all_gather(table, ("group", "dp", "head"), axis=0, tiled=False)
    table = table.reshape(n_group, n_dp, n_head, rows, EXPERTS)

    cached = latent_cache[0]
    scores = (
        jnp.einsum("rhc,rlc->rhl", queries[0], cached, preferred_element_type=f32) * softmax_scale
    )
    visible = lax.broadcasted_iota(jnp.int32, (reqs, 1, span), 2) < lengths[0][:, None, None]
    scores = jnp.where(visible, scores, -jnp.inf)
    row_max = jnp.max(scores, axis=2, keepdims=True)
    weights = jnp.exp(scores - row_max)
    shares = (weights / jnp.sum(weights, axis=2, keepdims=True)).astype(bf16)
    latent = jnp.einsum(
        "rhl,rlc->rhc", shares, cached[:, :, :latent_width], preferred_element_type=f32
    ).astype(bf16)
    head_rows = jnp.einsum("rhc,hcv->hrv", latent, w_value, preferred_element_type=f32).astype(bf16)

    res = residual[0].reshape(rows, n_dp, cols).transpose(1, 0, 2).reshape(n_dp, -1, value_width)
    res_rows = res.shape[1]
    pad = -res_rows % 16
    send = jnp.concatenate(
        [
            jnp.broadcast_to(
                head_rows.reshape(1, heads * reqs, value_width),
                (n_dp, heads * reqs, value_width),
            ),
            jnp.pad(res, ((0, 0), (0, pad), (0, 0))),
        ],
        axis=1,
    )
    got = lax.all_to_all(send, "dp", split_axis=0, concat_axis=0, tiled=True)
    res_piece = got[:, heads * reqs : heads * reqs + res_rows].reshape(n_dp * rows, cols)
    values = got[:, : heads * reqs].reshape(n_dp, heads, n_head, rows, value_width)
    partial = jnp.einsum(
        "dhziv,hvc->zdic",
        values,
        w_out.reshape(heads, value_width, cols),
        preferred_element_type=f32,
    ).astype(bf16)
    partial = lax.all_to_all(
        partial.reshape(n_head, n_dp * rows, cols), "head", split_axis=0, concat_axis=0, tiled=True
    )
    attended = jnp.sum(partial.astype(f32), axis=0).astype(bf16)
    hidden_piece = (res_piece.astype(f32) + attended.astype(f32)).astype(bf16)

    hidden = lax.all_to_all(
        jnp.broadcast_to(hidden_piece[None], (n_dp,) + hidden_piece.shape),
        "dp",
        split_axis=0,
        concat_axis=0,
        tiled=True,
    )
    hidden = hidden.transpose(1, 0, 2).reshape(n_dp * rows, width)
    hidden_f = hidden.astype(f32)
    mean_square = jnp.mean(hidden_f * hidden_f, axis=1, keepdims=True)
    normed = (hidden_f * lax.rsqrt(mean_square + norm_eps) * norm_gain).astype(bf16)
    home = lax.dynamic_slice(hidden, (dp * rows, 0), (rows, width))

    slot_ids = jnp.arange(CAP, dtype=jnp.int32)
    mine = lax.dynamic_index_in_dim(lax.dynamic_index_in_dim(table, g, 0, False), z, 1, False)
    mine = lax.dynamic_index_in_dim(mine, dp, 2, False) > 0
    before = jnp.cumsum(mine.astype(jnp.int32), axis=1) - mine
    placed = mine[:, None, :] & (before[:, None, :] == slot_ids[None, :, None])
    same = jnp.eye(n_dp, dtype=bool)
    pack = (placed[:, :, None, :] & same[:, None, :, None]).reshape(n_dp * CAP, n_dp * rows)
    packed = jnp.dot(pack.astype(bf16), normed, preferred_element_type=f32).astype(bf16)
    block = lax.all_gather(packed, ("group", "head"), axis=0, tiled=True)

    gate = jnp.dot(block, w_gate[0], preferred_element_type=f32)
    upward = jnp.dot(block, w_up[0], preferred_element_type=f32)
    active = (jax.nn.silu(gate) * upward).astype(bf16)
    active = (
        active.reshape(n_col, n_dp, CAP, -1).transpose(1, 0, 2, 3).reshape(n_col * n_dp * CAP, -1)
    )
    actives = lax.all_gather(active, ("group", "head"), axis=0, tiled=False)
    out = jnp.einsum("srf,scf->rc", actives, down, preferred_element_type=f32).astype(bf16)
    back = lax.all_to_all(
        out.reshape(n_dp, n_col * CAP, piece), "dp", split_axis=0, concat_axis=0, tiled=True
    )

    ours = lax.dynamic_index_in_dim(table, dp, 1, False).reshape(n_col, rows, EXPERTS)
    taken = ours > 0
    ahead = jnp.cumsum(taken.astype(jnp.int32), axis=1) - taken
    spread = jnp.where(
        taken[..., None] & (ahead[..., None] == slot_ids), ours[..., None], 0.0
    )
    mix = jnp.where(
        jnp.eye(n_col, dtype=bool)[:, None, None, :, None], spread[:, :, :, None, :], 0.0
    ).reshape(n_col * rows, EXPERTS * n_col * CAP)
    mix_high = mix.astype(bf16)
    mix_low = (mix - mix_high.astype(f32)).astype(bf16)
    back = back.reshape(EXPERTS * n_col * CAP, piece)
    mixed = jnp.dot(mix_high, back, preferred_element_type=f32) + jnp.dot(
        mix_low, back, preferred_element_type=f32
    )
    mixed = lax.all_to_all(
        mixed.astype(bf16).reshape(n_col, rows, piece),
        ("group", "head"),
        split_axis=0,
        concat_axis=0,
        tiled=True,
    )
    mixture = mixed.transpose(1, 0, 2).reshape(rows, width)
    layer_out = (home.astype(f32) + mixture.astype(f32)).astype(bf16)
    return layer_out[None]


def solution(mesh):
    in_specs = (
        P("group", "dp", "head", None),
        P("group", "dp", None, None),
        P("group", "dp"),
        P("head", None, None),
        P("head", "dp"),
        P("group", ("dp", "head"), None),
        P(),
        P("group", ("dp", "head"), None),
        P("group", ("dp", "head"), None),
        P("dp", None, ("group", "head")),
        P("dp", None, ("group", "head")),
        P("dp", None, ("group", "head")),
    )
    out_specs = P("group", ("dp", "head"), None)
    return jax.shard_map(local, mesh=mesh, in_specs=in_specs, out_specs=out_specs, check_vma=False)
```

```python
import jax
import jax.numpy as jnp
from jax import lax
from jax.sharding import PartitionSpec as P

EXPERTS = 16
CAP = 3


softmax_scale = 0.07216878364870323
norm_eps = 1e-06
bf16 = jnp.bfloat16
f32 = jnp.float32


def local(
    queries,
    latent_cache,
    lengths,
    w_value,
    w_out,
    residual,
    norm_gain,
    routes,
    gate_weights,
    w_gate,
    w_up,
    w_down,
):
    reqs = queries.shape[1]
    heads = queries.shape[2]
    latent_width = w_value.shape[1]
    value_width = w_value.shape[2]
    span = latent_cache.shape[2]
    rows = residual.shape[1]
    width = residual.shape[2]
    n_group = lax.axis_size("group")
    n_dp = lax.axis_size("dp")
    n_head = lax.axis_size("head")
    n_col = n_group * n_head
    cols = width // n_dp
    piece = width // n_col
    g = lax.axis_index("group")
    dp = lax.axis_index("dp")
    z = lax.axis_index("head")

    slabs = w_down[0].reshape(n_group, n_head, piece, w_down.shape[2])

    def shifted(k):
        slab = lax.dynamic_index_in_dim(slabs, lax.rem(z + k, n_head), 1, False)
        if k == 0:
            return slab
        return lax.ppermute(slab, "head", [(i, (i + k) % n_head) for i in range(n_head)])

    shifts = [shifted(k) for k in range(n_head)]

    expert_ids = jnp.arange(EXPERTS, dtype=jnp.int32)
    chosen = routes[0][:, :, None] == expert_ids[None, None, :]
    table = jnp.max(jnp.where(chosen, gate_weights[0][:, :, None], -1.0), axis=1)
    table_high = table.astype(bf16)
    table_low = (table - table_high.astype(f32)).astype(bf16)
    info = jnp.concatenate([table_high, table_low], axis=1)
    info = lax.all_to_all(
        jnp.broadcast_to(info[None], (n_col,) + info.shape),
        ("group", "head"),
        split_axis=0,
        concat_axis=0,
        tiled=True,
    ).reshape(n_col * rows, 2 * EXPERTS)

    cached = latent_cache[0]
    scores = (
        jnp.einsum("rhc,rlc->rhl", queries[0], cached, preferred_element_type=f32) * softmax_scale
    )
    visible = lax.broadcasted_iota(jnp.int32, (reqs, 1, span), 2) < lengths[0][:, None, None]
    scores = jnp.where(visible, scores, -jnp.inf)
    row_max = jnp.max(scores, axis=2, keepdims=True)
    weights = jnp.exp(scores - row_max)
    shares = (weights / jnp.sum(weights, axis=2, keepdims=True)).astype(bf16)
    latent = jnp.einsum(
        "rhl,rlc->rhc", shares, cached[:, :, :latent_width], preferred_element_type=f32
    ).astype(bf16)
    head_rows = jnp.einsum("rhc,hcv->hrv", latent, w_value, preferred_element_type=f32).astype(bf16)

    res = residual[0].reshape(rows, n_dp, cols).transpose(1, 0, 2).reshape(n_dp, -1, value_width)
    res_rows = res.shape[1]
    facts = jnp.pad(
        table_high.T[:, None, :], ((0, 0), (0, -res_rows % 16 - 1), (0, value_width - rows))
    )
    send = jnp.concatenate(
        [
            jnp.broadcast_to(
                head_rows.reshape(1, heads * reqs, value_width),
                (n_dp, heads * reqs, value_width),
            ),
            res,
            facts,
        ],
        axis=1,
    )
    send, info = lax.optimization_barrier((send, info))
    got = lax.all_to_all(send, "dp", split_axis=0, concat_axis=0, tiled=True)
    early = lax.optimization_barrier((got, shifts[1], shifts[7], shifts[2], shifts[6]))
    got, shifts[1], shifts[7], shifts[2], shifts[6] = early
    res_piece = got[:, heads * reqs : heads * reqs + res_rows].reshape(n_dp * rows, cols)
    mine = got[:, heads * reqs + res_rows, :rows].reshape(1, n_dp * rows) > 0
    values = got[:, : heads * reqs].reshape(n_dp, heads, n_head, rows, value_width)
    partial = jnp.einsum(
        "dhziv,hvc->zdic",
        values,
        w_out.reshape(heads, value_width, cols),
        preferred_element_type=f32,
    ).astype(bf16)
    partial = lax.all_to_all(
        partial.reshape(n_head, n_dp * rows, cols), "head", split_axis=0, concat_axis=0, tiled=True
    )
    attended = jnp.sum(partial.astype(f32), axis=0).astype(bf16)
    hidden_piece = (res_piece.astype(f32) + attended.astype(f32)).astype(bf16)

    hidden = lax.all_to_all(
        jnp.broadcast_to(hidden_piece[None], (n_dp,) + hidden_piece.shape),
        "dp",
        split_axis=0,
        concat_axis=0,
        tiled=True,
    )
    late = lax.optimization_barrier((hidden, shifts[3], shifts[5], shifts[4]))
    hidden, shifts[3], shifts[5], shifts[4] = late
    home = lax.dynamic_slice(hidden, (0, dp * rows, 0), (n_dp, rows, cols))
    hidden = hidden.transpose(1, 0, 2).reshape(n_dp * rows, width)
    hidden_f = hidden.astype(f32)
    mean_square = jnp.mean(hidden_f * hidden_f, axis=1, keepdims=True)
    normed = (hidden_f * lax.rsqrt(mean_square + norm_eps) * norm_gain).astype(bf16)

    def index(shape, axis):
        return lax.broadcasted_iota(jnp.int32, shape, axis)

    def before(count):
        a, b = index((count, count), 0), index((count, count), 1)
        return ((a // rows == b // rows) & (a < b)).astype(bf16)

    count = n_dp * rows
    slot = jnp.dot(mine.astype(bf16), before(count), preferred_element_type=f32)
    at, of = index((n_dp * CAP, count), 0), index((n_dp * CAP, count), 1)
    pack = (at // CAP == of // rows) & mine & (slot == (at % CAP).astype(f32))
    packed = jnp.dot(pack.astype(bf16), normed, preferred_element_type=f32).astype(bf16)
    block = lax.all_gather(packed, ("group", "head"), axis=0, tiled=True)

    gate = jnp.dot(block, w_gate[0], preferred_element_type=f32)
    upward = jnp.dot(block, w_up[0], preferred_element_type=f32)
    active = (jax.nn.silu(gate) * upward).astype(bf16)
    active = (
        active.reshape(n_col, n_dp, CAP, -1).transpose(1, 0, 2, 3).reshape(n_col * n_dp * CAP, -1)
    )
    actives = lax.all_gather(active, ("group", "head"), axis=0, tiled=False)
    stack = jnp.stack(shifts[::-1] + shifts[::-1])
    stack = lax.dynamic_slice_in_dim(stack, lax.rem(2 * n_head - 1 - z, n_head), n_head, 0)
    kept = lax.dynamic_index_in_dim(stack, g, 1, False)
    given = lax.dynamic_index_in_dim(stack, 1 - g, 1, False)
    given = lax.ppermute(given, "group", [(0, 1), (1, 0)])
    down = jnp.where(g == 0, jnp.concatenate([kept, given]), jnp.concatenate([given, kept]))
    out = jnp.einsum("srf,scf->rc", actives, down, preferred_element_type=f32).astype(bf16)
    back = lax.all_to_all(
        out.reshape(n_dp, n_col * CAP, piece), "dp", split_axis=0, concat_axis=0, tiled=True
    )

    ours_high, ours_low = info[:, :EXPERTS], info[:, EXPERTS:]
    taken = (ours_high > 0).astype(bf16)
    count = n_col * rows
    ahead = jnp.dot(before(count).T, taken, preferred_element_type=f32)
    ahead = jnp.where(taken > 0, ahead, -1.0).astype(bf16)
    wide = EXPERTS * n_col * CAP
    spread = (index((EXPERTS, wide), 0) == index((EXPERTS, wide), 1) // (n_col * CAP)).astype(bf16)
    at, of = index((count, wide), 0), index((count, wide), 1)
    hit = (at // rows == of // CAP % n_col) & (
        jnp.dot(ahead, spread, preferred_element_type=f32) == (of % CAP).astype(f32)
    )
    zero = jnp.zeros((), f32)
    mix_high = jnp.where(
        hit, jnp.dot(ours_high, spread, preferred_element_type=f32), zero
    ).astype(bf16)
    mix_low = jnp.where(
        hit, jnp.dot(ours_low, spread, preferred_element_type=f32), zero
    ).astype(bf16)
    back = back.reshape(EXPERTS * n_col * CAP, piece)
    mixed = jnp.dot(mix_high, back, preferred_element_type=f32) + jnp.dot(
        mix_low, back, preferred_element_type=f32
    )
    mixed = lax.all_to_all(
        mixed.astype(bf16).reshape(n_col, rows, piece),
        ("group", "head"),
        split_axis=0,
        concat_axis=0,
        tiled=True,
    )
    layer_out = (home.astype(f32) + mixed.astype(f32)).astype(bf16)
    layer_out = layer_out.transpose(1, 0, 2).reshape(rows, width)
    return layer_out[None]


def solution(mesh):
    in_specs = (
        P("group", "dp", "head", None),
        P("group", "dp", None, None),
        P("group", "dp"),
        P("head", None, None),
        P("head", "dp"),
        P("group", ("dp", "head"), None),
        P(),
        P("group", ("dp", "head"), None),
        P("group", ("dp", "head"), None),
        P("dp", None, ("group", "head")),
        P("dp", None, ("group", "head")),
        P("dp", None, ("group", "head")),
    )
    out_specs = P("group", ("dp", "head"), None)
    return jax.shard_map(local, mesh=mesh, in_specs=in_specs, out_specs=out_specs, check_vma=False)
```

```python
import functools

import jax
import jax.numpy as jnp
from jax import lax
from jax.experimental import pallas as pl
from jax.experimental.pallas import tpu as pltpu
from jax.sharding import PartitionSpec as P

EXPERTS = 16
CAP = 3


softmax_scale = 0.07216878364870323
norm_eps = 1e-06
bf16 = jnp.bfloat16
f32 = jnp.float32


VMEM = pl.BlockSpec(memory_space=pltpu.VMEM)
SMEM = pl.BlockSpec(memory_space=pltpu.SMEM)
LANES = 128


def norm_pack_kernel(hidden_ref, gain_ref, pack_ref, extra_ref, out_ref):
    parts, count, cols = hidden_ref.shape
    square = jnp.zeros((count, 1), f32)
    for p in range(parts):
        part = hidden_ref[p].astype(f32)
        square += jnp.sum(part * part, axis=1, keepdims=True)
    scale = lax.rsqrt(square / (parts * cols) + norm_eps)
    pack = pack_ref[...]
    for p in range(parts):
        normed = (hidden_ref[p].astype(f32) * scale * gain_ref[p : p + 1]).astype(bf16)
        rows = jnp.dot(pack, normed, preferred_element_type=f32).astype(bf16)
        out_ref[:, p * cols : (p + 1) * cols] = rows
    extra = jnp.dot(pack, extra_ref[...], preferred_element_type=f32).astype(bf16)
    out_ref[:, parts * cols :] = extra


def norm_pack(hidden, gain, pack, extra):
    parts, _, cols = hidden.shape
    return pl.pallas_call(
        norm_pack_kernel,
        out_shape=jax.ShapeDtypeStruct((pack.shape[0], parts * cols + LANES), bf16),
        in_specs=[VMEM] * 4,
        out_specs=VMEM,
        compiler_params=pltpu.CompilerParams(vmem_limit_bytes=32 << 20),
    )(hidden, gain, pack, extra)


def gate_up_kernel(count, *refs):
    blocks, (gate_ref, up_ref, out_ref) = refs[:count], refs[count:]
    width = gate_ref.shape[0]
    step = 1024
    gate = up = 0.0
    for k in range(0, width, step):
        rows = jnp.concatenate([b[:, k : k + step] for b in blocks], axis=0)
        gate += jnp.dot(rows, gate_ref[k : k + step], preferred_element_type=f32)
        up += jnp.dot(rows, up_ref[k : k + step], preferred_element_type=f32)
    out_ref[:, :LANES] = (gate / (1.0 + jnp.exp(-gate)) * up).astype(bf16)
    out_ref[:, LANES:] = jnp.concatenate([b[:, width:] for b in blocks], axis=0)


def gate_up(blocks, w_gate, w_up):
    rows = sum(b.shape[0] for b in blocks)
    return pl.pallas_call(
        functools.partial(gate_up_kernel, len(blocks)),
        out_shape=jax.ShapeDtypeStruct((rows, 2 * LANES), bf16),
        in_specs=[VMEM] * (len(blocks) + 2),
        out_specs=VMEM,
        compiler_params=pltpu.CompilerParams(vmem_limit_bytes=32 << 20),
    )(*blocks, w_gate, w_up)


def down_kernel(count, *refs):
    g_ref, refs = refs[0], refs[1:]
    actives, downs, (keep_ref, give_ref) = refs[:count], refs[count : 2 * count], refs[2 * count :]
    g = g_ref[0]
    step = 256
    for at, out_ref in ((g, keep_ref), (1 - g, give_ref)):
        weights = [
            jnp.concatenate([downs[k][at], downs[k + 1][at]], axis=1) for k in range(0, count, 2)
        ]
        for r in range(0, keep_ref.shape[0], step):
            total = 0.0
            for k in range(0, count, 2):
                left = jnp.concatenate(
                    [actives[k][r : r + step], actives[k + 1][r : r + step]], axis=1
                )
                total += lax.dot_general(
                    left, weights[k // 2], (((1,), (1,)), ((), ())), preferred_element_type=f32
                )
            out_ref[r : r + step] = total.astype(out_ref.dtype)


def down_sums(g, actives, downs):
    shape = (actives[0].shape[0], downs[0].shape[1])
    return pl.pallas_call(
        functools.partial(down_kernel, len(actives)),
        out_shape=(jax.ShapeDtypeStruct(shape, f32), jax.ShapeDtypeStruct(shape, bf16)),
        in_specs=[SMEM] + [VMEM] * (2 * len(actives)),
        out_specs=(VMEM, VMEM),
        compiler_params=pltpu.CompilerParams(vmem_limit_bytes=32 << 20),
    )(g.reshape(1), *actives, *downs)


def ring(block, count, half):
    right = [(i, (i + 1) % count) for i in range(count)]
    left = [(i, (i - 1) % count) for i in range(count)]
    steps = []
    up = down = block
    for _ in range(count // 2 - 1):
        up = lax.ppermute(up, "head", right)
        down = lax.ppermute(down, "head", left)
        steps.append((up, down))
    last = (lax.ppermute(up[:half], "head", right), lax.ppermute(down[half:], "head", left))
    return steps, last


def local(
    queries,
    latent_cache,
    lengths,
    w_value,
    w_out,
    residual,
    norm_gain,
    routes,
    gate_weights,
    w_gate,
    w_up,
    w_down,
):
    reqs = queries.shape[1]
    heads = queries.shape[2]
    latent_width = w_value.shape[1]
    value_width = w_value.shape[2]
    span = latent_cache.shape[2]
    rows = residual.shape[1]
    width = residual.shape[2]
    n_group = lax.axis_size("group")
    n_dp = lax.axis_size("dp")
    n_head = lax.axis_size("head")
    n_col = n_group * n_head
    cols = width // n_dp
    piece = width // n_col
    g = lax.axis_index("group")
    dp = lax.axis_index("dp")
    z = lax.axis_index("head")

    slabs = w_down[0].reshape(n_group, n_head, piece, w_down.shape[2])

    def shifted(k):
        slab = lax.dynamic_index_in_dim(slabs, lax.rem(z + k, n_head), 1, False)
        if k == 0:
            return slab
        return lax.ppermute(slab, "head", [(i, (i + k) % n_head) for i in range(n_head)])

    shifts = [shifted(k) for k in range(n_head)]

    expert_ids = jnp.arange(EXPERTS, dtype=jnp.int32)
    chosen = routes[0][:, :, None] == expert_ids[None, None, :]
    table = jnp.max(jnp.where(chosen, gate_weights[0][:, :, None], -1.0), axis=1)
    table_high = table.astype(bf16)
    table_low = (table - table_high.astype(f32)).astype(bf16)

    cached = latent_cache[0]
    scores = (
        jnp.einsum("rhc,rlc->rhl", queries[0], cached, preferred_element_type=f32) * softmax_scale
    )
    visible = lax.broadcasted_iota(jnp.int32, (reqs, 1, span), 2) < lengths[0][:, None, None]
    scores = jnp.where(visible, scores, -jnp.inf)
    row_max = jnp.max(scores, axis=2, keepdims=True)
    weights = jnp.exp(scores - row_max)
    shares = (weights / jnp.sum(weights, axis=2, keepdims=True)).astype(bf16)
    latent = jnp.einsum(
        "rhl,rlc->rhc", shares, cached[:, :, :latent_width], preferred_element_type=f32
    ).astype(bf16)
    head_rows = jnp.einsum("rhc,hcv->hrv", latent, w_value, preferred_element_type=f32).astype(bf16)

    res = residual[0].reshape(rows, n_dp, cols).transpose(1, 0, 2).reshape(n_dp, -1, value_width)
    res_rows = res.shape[1]
    facts = jnp.stack([table_high.T, table_low.T], axis=1)
    facts = jnp.pad(facts, ((0, 0), (0, -res_rows % 16 - 2), (0, value_width - rows)))
    send = jnp.concatenate(
        [
            jnp.broadcast_to(
                head_rows.reshape(1, heads * reqs, value_width),
                (n_dp, heads * reqs, value_width),
            ),
            res,
            facts,
        ],
        axis=1,
    )
    got = lax.all_to_all(send, "dp", split_axis=0, concat_axis=0, tiled=True)
    early = lax.optimization_barrier((got, shifts[1], shifts[7], shifts[2], shifts[6]))
    got, shifts[1], shifts[7], shifts[2], shifts[6] = early
    res_piece = got[:, heads * reqs : heads * reqs + res_rows].reshape(n_dp * rows, cols)
    fact = got[:, heads * reqs + res_rows :, :rows]
    mine = fact[:, 0].reshape(1, n_dp * rows) > 0
    values = got[:, : heads * reqs].reshape(n_dp, heads, n_head, rows, value_width)
    partial = jnp.einsum(
        "dhziv,hvc->zdic",
        values,
        w_out.reshape(heads, value_width, cols),
        preferred_element_type=f32,
    ).astype(bf16)
    partial = lax.all_to_all(
        partial.reshape(n_head, n_dp * rows, cols), "head", split_axis=0, concat_axis=0, tiled=True
    )
    attended = jnp.sum(partial.astype(f32), axis=0).astype(bf16)
    hidden_piece = (res_piece.astype(f32) + attended.astype(f32)).astype(bf16)

    hidden = lax.all_to_all(
        jnp.broadcast_to(hidden_piece[None], (n_dp,) + hidden_piece.shape),
        "dp",
        split_axis=0,
        concat_axis=0,
        tiled=True,
    )
    late = lax.optimization_barrier((hidden, shifts[3], shifts[5], shifts[4]))
    hidden, shifts[3], shifts[5], shifts[4] = late
    home = lax.dynamic_slice(hidden, (0, dp * rows, 0), (n_dp, rows, cols))

    def index(shape, axis):
        return lax.broadcasted_iota(jnp.int32, shape, axis)

    def before(count):
        a, b = index((count, count), 0), index((count, count), 1)
        return ((a // rows == b // rows) & (a < b)).astype(bf16)

    count = n_dp * rows
    slot = jnp.dot(mine.astype(bf16), before(count), preferred_element_type=f32)
    at, of = index((n_dp * CAP, count), 0), index((n_dp * CAP, count), 1)
    pack = (at // CAP == of // rows) & mine & (slot == (at % CAP).astype(f32))
    extra = jnp.concatenate(
        [
            fact[:, :2].transpose(0, 2, 1).reshape(count, 2),
            (index((count, 1), 0) % rows).astype(bf16),
            jnp.zeros((count, LANES - 3), bf16),
        ],
        axis=1,
    )
    packed = norm_pack(hidden, norm_gain.reshape(n_dp, cols), pack.astype(bf16), extra)

    def swap(block):
        return lax.ppermute(block, "group", [(0, 1), (1, 0)])

    fill = n_dp * CAP
    steps, last = ring(packed, n_head, fill // 2)
    groups = [(packed,)] + steps + [last]
    done = [gate_up(own + tuple(swap(b) for b in own), w_gate[0], w_up[0]) for own in groups]
    active = jnp.concatenate(done, axis=0)

    r = index((1, n_col * fill), 1)
    first, final = 2 * fill, (n_col - 2) * fill
    at = jnp.where(r < first, 0, (r - first) // (4 * fill) + 1)
    within = jnp.where(r < first, r, (r - first) % (4 * fill))
    other = jnp.where((r < first) | (r >= final), within // fill, within // (2 * fill))
    leftward = jnp.where((r < first) | (r >= final), 0, within // fill % 2)
    from_z = jnp.where(leftward == 1, z + at, z - at + n_head) % n_head
    from_g = jnp.where(other == 1, 1 - g, g)
    home_dp, place = r % fill // CAP, r % CAP
    to = home_dp * (n_col * CAP) + (from_g * n_head + from_z) * CAP + place
    order = (index((n_col * fill, n_col * fill), 0) == to).astype(bf16)
    active = jnp.dot(order, active, preferred_element_type=f32).astype(bf16)
    row_facts = active[:, LANES:].astype(f32)
    active = active[:, :LANES]

    steps, last = ring(active, n_head, n_col * fill // 2)
    far = jnp.concatenate(last, axis=0)
    actives = [active] + [s[0] for s in steps] + [far] + [s[1] for s in steps[::-1]]
    keep, give = down_sums(g, actives, shifts)
    out = ((keep + swap(give).astype(f32)) * (row_facts[:, :1] + row_facts[:, 1:2])).astype(bf16)
    out = jnp.concatenate(
        [out, row_facts[:, 2:3].astype(bf16), jnp.zeros((out.shape[0], 63), bf16)], axis=1
    )
    out = out.reshape(n_dp, n_col * CAP, -1)
    back = lax.all_to_all(out, "dp", split_axis=0, concat_axis=0, tiled=True)

    back = back.reshape(EXPERTS * n_col * CAP, -1)
    token = index((back.shape[0], 1), 0) // CAP % n_col * rows
    token = token.astype(f32) + back[:, piece : piece + 1].astype(f32)
    hit = token == index((back.shape[0], n_col * rows), 1).astype(f32)
    mixed = lax.dot_general(
        hit.astype(bf16),
        back[:, :piece],
        (((0,), (0,)), ((), ())),
        preferred_element_type=f32,
    )
    mixed = lax.all_to_all(
        mixed.astype(bf16).reshape(n_col, rows, piece),
        ("group", "head"),
        split_axis=0,
        concat_axis=0,
        tiled=True,
    )
    layer_out = (home.astype(f32) + mixed.astype(f32)).astype(bf16)
    layer_out = layer_out.transpose(1, 0, 2).reshape(rows, width)
    return layer_out[None]


def solution(mesh):
    in_specs = (
        P("group", "dp", "head", None),
        P("group", "dp", None, None),
        P("group", "dp"),
        P("head", None, None),
        P("head", "dp"),
        P("group", ("dp", "head"), None),
        P(),
        P("group", ("dp", "head"), None),
        P("group", ("dp", "head"), None),
        P("dp", None, ("group", "head")),
        P("dp", None, ("group", "head")),
        P("dp", None, ("group", "head")),
    )
    out_specs = P("group", ("dp", "head"), None)
    return jax.shard_map(local, mesh=mesh, in_specs=in_specs, out_specs=out_specs, check_vma=False)
```

```python
import functools

import jax
import jax.numpy as jnp
from jax import lax
from jax.experimental import pallas as pl
from jax.experimental.pallas import tpu as pltpu
from jax.sharding import PartitionSpec as P

EXPERTS = 16
CAP = 3


softmax_scale = 0.07216878364870323
norm_eps = 1e-06
bf16 = jnp.bfloat16
f32 = jnp.float32


VMEM = pl.BlockSpec(memory_space=pltpu.VMEM)
SMEM = pl.BlockSpec(memory_space=pltpu.SMEM)
LANES = 128


def norm_pack_kernel(hidden_ref, gain_ref, pack_ref, extra_ref, out_ref):
    parts, count, cols = hidden_ref.shape
    square = jnp.zeros((count, 1), f32)
    for p in range(parts):
        part = hidden_ref[p].astype(f32)
        square += jnp.sum(part * part, axis=1, keepdims=True)
    scale = lax.rsqrt(square / (parts * cols) + norm_eps)
    pack = pack_ref[...]
    for p in range(parts):
        normed = (hidden_ref[p].astype(f32) * scale * gain_ref[p : p + 1]).astype(bf16)
        rows = jnp.dot(pack, normed, preferred_element_type=f32).astype(bf16)
        out_ref[:, p * cols : (p + 1) * cols] = rows
    extra = jnp.dot(pack, extra_ref[...], preferred_element_type=f32).astype(bf16)
    out_ref[:, parts * cols :] = extra


def norm_pack(hidden, gain, pack, extra):
    parts, _, cols = hidden.shape
    return pl.pallas_call(
        norm_pack_kernel,
        out_shape=jax.ShapeDtypeStruct((pack.shape[0], parts * cols + LANES), bf16),
        in_specs=[VMEM] * 4,
        out_specs=VMEM,
        compiler_params=pltpu.CompilerParams(vmem_limit_bytes=32 << 20),
    )(hidden, gain, pack, extra)


def gate_up_kernel(count, *refs):
    blocks, (gate_ref, up_ref, out_ref) = refs[:count], refs[count:]
    width = gate_ref.shape[0]
    step = 1024
    gate = up = 0.0
    for k in range(0, width, step):
        rows = jnp.concatenate([b[:, k : k + step] for b in blocks], axis=0)
        gate += jnp.dot(rows, gate_ref[k : k + step], preferred_element_type=f32)
        up += jnp.dot(rows, up_ref[k : k + step], preferred_element_type=f32)
    out_ref[:, :LANES] = (gate / (1.0 + jnp.exp(-gate)) * up).astype(bf16)
    out_ref[:, LANES:] = jnp.concatenate([b[:, width:] for b in blocks], axis=0)


def gate_up(blocks, w_gate, w_up):
    rows = sum(b.shape[0] for b in blocks)
    return pl.pallas_call(
        functools.partial(gate_up_kernel, len(blocks)),
        out_shape=jax.ShapeDtypeStruct((rows, 2 * LANES), bf16),
        in_specs=[VMEM] * (len(blocks) + 2),
        out_specs=VMEM,
        compiler_params=pltpu.CompilerParams(vmem_limit_bytes=32 << 20),
    )(*blocks, w_gate, w_up)


def down_kernel(count, *refs):
    g_ref, refs = refs[0], refs[1:]
    actives, downs, (keep_ref, give_ref) = refs[:count], refs[count : 2 * count], refs[2 * count :]
    g = g_ref[0]
    step = 256
    for at, out_ref in ((g, keep_ref), (1 - g, give_ref)):
        weights = [
            jnp.concatenate([downs[k][at], downs[k + 1][at]], axis=1) for k in range(0, count, 2)
        ]
        for r in range(0, keep_ref.shape[0], step):
            total = 0.0
            for k in range(0, count, 2):
                left = jnp.concatenate(
                    [actives[k][r : r + step], actives[k + 1][r : r + step]], axis=1
                )
                total += lax.dot_general(
                    left, weights[k // 2], (((1,), (1,)), ((), ())), preferred_element_type=f32
                )
            out_ref[r : r + step] = total.astype(out_ref.dtype)


def down_sums(g, actives, downs):
    shape = (actives[0].shape[0], downs[0].shape[1])
    return pl.pallas_call(
        functools.partial(down_kernel, len(actives)),
        out_shape=(jax.ShapeDtypeStruct(shape, f32), jax.ShapeDtypeStruct(shape, bf16)),
        in_specs=[SMEM] + [VMEM] * (2 * len(actives)),
        out_specs=(VMEM, VMEM),
        compiler_params=pltpu.CompilerParams(vmem_limit_bytes=32 << 20),
    )(g.reshape(1), *actives, *downs)


def combine_kernel(keep_ref, got_ref, facts_ref, out_ref):
    facts = facts_ref[...].astype(f32)
    cols = keep_ref.shape[1]
    total = (keep_ref[...] + got_ref[...].astype(f32)) * (facts[:, :1] + facts[:, 1:2])
    out_ref[:, :cols] = total.astype(bf16)
    rest = out_ref.shape[1] - cols
    out_ref[:, cols:] = jnp.broadcast_to(facts[:, 2:3], (facts.shape[0], rest)).astype(bf16)


def combine(keep, got, facts):
    rows, cols = keep.shape
    return pl.pallas_call(
        combine_kernel,
        out_shape=jax.ShapeDtypeStruct((rows, cols + -cols % LANES), bf16),
        in_specs=[VMEM] * 3,
        out_specs=VMEM,
        compiler_params=pltpu.CompilerParams(vmem_limit_bytes=32 << 20),
    )(keep, got, facts)


def ring(block, beside):
    count, cores = lax.axis_size("head"), lax.axis_size("group")
    right = [(i, (i + 1) % count) for i in range(count)]
    left = [(i, (i - 1) % count) for i in range(count)]
    both = [
        (c * count + i, c * count + (i + 1 - 2 * c) % count)
        for c in range(cores)
        for i in range(count)
    ]
    steps, results = [(block,)], []
    for step in range(count // 2):
        held = steps[-1]
        if step < count // 2 - 1:
            got = (lax.ppermute(held[0], "head", right), lax.ppermute(held[-1], "head", left))
        else:
            one = jnp.where(lax.axis_index("group") == 0, held[0], held[-1])
            got = (lax.ppermute(one, ("group", "head"), both),)
        if beside is not None:
            result = beside(held)
            got, result = lax.optimization_barrier((got, result))
            results.append(result)
        steps.append(got)
    if beside is not None:
        results.append(beside(steps[-1]))
    return steps, results


def local(
    queries,
    latent_cache,
    lengths,
    w_value,
    w_out,
    residual,
    norm_gain,
    routes,
    gate_weights,
    w_gate,
    w_up,
    w_down,
):
    reqs = queries.shape[1]
    heads = queries.shape[2]
    latent_width = w_value.shape[1]
    value_width = w_value.shape[2]
    span = latent_cache.shape[2]
    rows = residual.shape[1]
    width = residual.shape[2]
    n_group = lax.axis_size("group")
    n_dp = lax.axis_size("dp")
    n_head = lax.axis_size("head")
    n_col = n_group * n_head
    cols = width // n_dp
    piece = width // n_col
    g = lax.axis_index("group")
    dp = lax.axis_index("dp")
    z = lax.axis_index("head")

    slabs = w_down[0].reshape(n_group, n_head, piece, w_down.shape[2])
    slabs = [
        lax.dynamic_index_in_dim(slabs, lax.rem(z + k, n_head), 1, False) for k in range(n_head)
    ]
    shifts = [slabs[0]] + [None] * (n_head - 1)

    def shift(some):
        for k in some:
            shifts[k] = lax.ppermute(
                slabs[k], "head", [(i, (i + k) % n_head) for i in range(n_head)]
            )

    expert_ids = jnp.arange(EXPERTS, dtype=jnp.int32)
    chosen = routes[0][:, :, None] == expert_ids[None, None, :]
    table = jnp.max(jnp.where(chosen, gate_weights[0][:, :, None], -1.0), axis=1)
    table_high = table.astype(bf16)
    table_low = (table - table_high.astype(f32)).astype(bf16)

    cached = latent_cache[0]
    scores = (
        jnp.einsum("rhc,rlc->rhl", queries[0], cached, preferred_element_type=f32) * softmax_scale
    )
    visible = lax.broadcasted_iota(jnp.int32, (reqs, 1, span), 2) < lengths[0][:, None, None]
    scores = jnp.where(visible, scores, -jnp.inf)
    row_max = jnp.max(scores, axis=2, keepdims=True)
    weights = jnp.exp(scores - row_max)
    shares = (weights / jnp.sum(weights, axis=2, keepdims=True)).astype(bf16)
    latent = jnp.einsum(
        "rhl,rlc->rhc", shares, cached[:, :, :latent_width], preferred_element_type=f32
    ).astype(bf16)
    head_rows = jnp.einsum("rhc,hcv->hrv", latent, w_value, preferred_element_type=f32).astype(bf16)

    res = residual[0].reshape(rows, n_dp, cols).transpose(1, 0, 2).reshape(n_dp, -1, value_width)
    res_rows = res.shape[1]
    facts = jnp.stack([table_high.T, table_low.T], axis=1)
    facts = jnp.pad(facts, ((0, 0), (0, -res_rows % 16 - 2), (0, value_width - rows)))
    send = jnp.concatenate(
        [
            jnp.broadcast_to(
                head_rows.reshape(1, heads * reqs, value_width),
                (n_dp, heads * reqs, value_width),
            ),
            res,
            facts,
        ],
        axis=1,
    )
    got = lax.all_to_all(send, "dp", split_axis=0, concat_axis=0, tiled=True)
    shift((3, 5, 1, 7))
    early = lax.optimization_barrier((got, shifts[3], shifts[5], shifts[1], shifts[7]))
    got, shifts[3], shifts[5], shifts[1], shifts[7] = early
    res_piece = got[:, heads * reqs : heads * reqs + res_rows].reshape(n_dp * rows, cols)
    fact = got[:, heads * reqs + res_rows :, :rows]
    mine = fact[:, 0].reshape(1, n_dp * rows) > 0
    values = got[:, : heads * reqs].reshape(n_dp, heads, n_head, rows, value_width)
    partial = jnp.einsum(
        "dhziv,hvc->zdic",
        values,
        w_out.reshape(heads, value_width, cols),
        preferred_element_type=f32,
    ).astype(bf16)
    partial = lax.all_to_all(
        partial.reshape(n_head, n_dp * rows, cols), "head", split_axis=0, concat_axis=0, tiled=True
    )
    held = lax.optimization_barrier((partial, slabs[4], slabs[2], slabs[6]))
    partial, slabs[4], slabs[2], slabs[6] = held
    attended = jnp.sum(partial.astype(f32), axis=0).astype(bf16)
    hidden_piece = (res_piece.astype(f32) + attended.astype(f32)).astype(bf16)

    hidden = lax.all_to_all(
        jnp.broadcast_to(hidden_piece[None], (n_dp,) + hidden_piece.shape),
        "dp",
        split_axis=0,
        concat_axis=0,
        tiled=True,
    )
    shift((4, 2, 6))
    late = lax.optimization_barrier((hidden, shifts[4], shifts[2], shifts[6]))
    hidden, shifts[4], shifts[2], shifts[6] = late
    home = lax.dynamic_slice(hidden, (0, dp * rows, 0), (n_dp, rows, cols))

    def index(shape, axis):
        return lax.broadcasted_iota(jnp.int32, shape, axis)

    def before(count):
        a, b = index((count, count), 0), index((count, count), 1)
        return ((a // rows == b // rows) & (a < b)).astype(bf16)

    count = n_dp * rows
    slot = jnp.dot(mine.astype(bf16), before(count), preferred_element_type=f32)
    at, of = index((n_dp * CAP, count), 0), index((n_dp * CAP, count), 1)
    pack = (at // CAP == of // rows) & mine & (slot == (at % CAP).astype(f32))
    extra = jnp.concatenate(
        [
            fact[:, :2].transpose(0, 2, 1).reshape(count, 2),
            (index((count, 1), 0) % rows).astype(bf16),
            jnp.zeros((count, LANES - 3), bf16),
        ],
        axis=1,
    )
    packed = norm_pack(hidden, norm_gain.reshape(n_dp, cols), pack.astype(bf16), extra)

    def swap(block):
        return lax.ppermute(block, "group", [(0, 1), (1, 0)])

    fill = n_dp * CAP
    def work(blocks):
        return gate_up(blocks + tuple(swap(b) for b in blocks), w_gate[0], w_up[0])

    _, done = ring(packed, work)
    active = jnp.concatenate(done, axis=0)

    r = index((1, n_col * fill), 1)
    first, final = 2 * fill, (n_col - 2) * fill
    at = jnp.where(r < first, 0, (r - first) // (4 * fill) + 1)
    within = jnp.where(r < first, r, (r - first) % (4 * fill))
    other = jnp.where((r < first) | (r >= final), within // fill, within // (2 * fill))
    leftward = jnp.where((r < first) | (r >= final), 0, within // fill % 2)
    from_z = jnp.where(leftward == 1, z + at, z - at + n_head) % n_head
    from_g = jnp.where(other == 1, 1 - g, g)
    home_dp, place = r % fill // CAP, r % CAP
    to = home_dp * (n_col * CAP) + (from_g * n_head + from_z) * CAP + place
    order = (index((n_col * fill, n_col * fill), 0) == to).astype(bf16)
    active = jnp.dot(order, active, preferred_element_type=f32).astype(bf16)
    row_facts = active[:, LANES:]
    active = active[:, :LANES]

    steps, _ = ring(active, None)
    actives = [s[0] for s in steps] + [s[1] for s in steps[-2:0:-1]]
    keep, give = down_sums(g, actives, shifts)
    out = combine(keep, swap(give), row_facts).reshape(n_dp, n_col * CAP, -1)
    back = lax.all_to_all(out, "dp", split_axis=0, concat_axis=0, tiled=True)

    back = back.reshape(EXPERTS * n_col * CAP, -1)
    token = index((back.shape[0], 1), 0) // CAP % n_col * rows
    token = token.astype(f32) + back[:, piece : piece + 1].astype(f32)
    hit = token == index((back.shape[0], n_col * rows), 1).astype(f32)
    mixed = lax.dot_general(
        hit.astype(bf16),
        back[:, :piece],
        (((0,), (0,)), ((), ())),
        preferred_element_type=f32,
    )
    mixed = lax.all_to_all(
        mixed.astype(bf16).reshape(n_col, rows, piece),
        ("group", "head"),
        split_axis=0,
        concat_axis=0,
        tiled=True,
    )
    layer_out = (home.astype(f32) + mixed.astype(f32)).astype(bf16)
    layer_out = layer_out.transpose(1, 0, 2).reshape(rows, width)
    return layer_out[None]


def solution(mesh):
    in_specs = (
        P("group", "dp", "head", None),
        P("group", "dp", None, None),
        P("group", "dp"),
        P("head", None, None),
        P("head", "dp"),
        P("group", ("dp", "head"), None),
        P(),
        P("group", ("dp", "head"), None),
        P("group", ("dp", "head"), None),
        P("dp", None, ("group", "head")),
        P("dp", None, ("group", "head")),
        P("dp", None, ("group", "head")),
    )
    out_specs = P("group", ("dp", "head"), None)
    return jax.shard_map(local, mesh=mesh, in_specs=in_specs, out_specs=out_specs, check_vma=False)
```

```python
import functools

import jax
import jax.numpy as jnp
from jax import lax
from jax.experimental import pallas as pl
from jax.experimental.pallas import tpu as pltpu
from jax.sharding import PartitionSpec as P

EXPERTS = 16
CAP = 3


softmax_scale = 0.07216878364870323
norm_eps = 1e-06
bf16 = jnp.bfloat16
f32 = jnp.float32


VMEM = pl.BlockSpec(memory_space=pltpu.VMEM)
SMEM = pl.BlockSpec(memory_space=pltpu.SMEM)
LANES = 128


def norm_pack_kernel(hidden_ref, gain_ref, pack_ref, extra_ref, out_ref):
    parts, count, cols = hidden_ref.shape
    square = jnp.zeros((count, 1), f32)
    for p in range(parts):
        part = hidden_ref[p].astype(f32)
        square += jnp.sum(part * part, axis=1, keepdims=True)
    scale = lax.rsqrt(square / (parts * cols) + norm_eps)
    pack = pack_ref[...]
    for p in range(parts):
        normed = (hidden_ref[p].astype(f32) * scale * gain_ref[p : p + 1]).astype(bf16)
        rows = jnp.dot(pack, normed, preferred_element_type=f32).astype(bf16)
        out_ref[:, p * cols : (p + 1) * cols] = rows
    extra = jnp.dot(pack, extra_ref[...], preferred_element_type=f32).astype(bf16)
    out_ref[:, parts * cols :] = extra


def norm_pack(hidden, gain, pack, extra):
    parts, _, cols = hidden.shape
    return pl.pallas_call(
        norm_pack_kernel,
        out_shape=jax.ShapeDtypeStruct((pack.shape[0], parts * cols + LANES), bf16),
        in_specs=[VMEM] * 4,
        out_specs=VMEM,
        compiler_params=pltpu.CompilerParams(vmem_limit_bytes=32 << 20),
    )(hidden, gain, pack, extra)


def gate_up_kernel(count, *refs):
    blocks, (gate_ref, gate2_ref, up_ref, up2_ref, out_ref) = refs[:count], refs[count:]
    width = gate_ref.shape[0]
    step = 1024
    gate = up = 0.0
    for k in range(0, width, step):
        rows = jnp.concatenate([b[:, k : k + step] for b in blocks], axis=0)
        weights = jnp.concatenate([gate_ref[k : k + step], gate2_ref[k : k + step]], axis=1)
        gate += jnp.dot(rows, weights, preferred_element_type=f32)
        weights = jnp.concatenate([up_ref[k : k + step], up2_ref[k : k + step]], axis=1)
        up += jnp.dot(rows, weights, preferred_element_type=f32)
    out_ref[:, : 2 * LANES] = (gate / (1.0 + jnp.exp(-gate)) * up).astype(bf16)
    out_ref[:, 2 * LANES :] = jnp.concatenate([b[:, width:] for b in blocks], axis=0)


def gate_up(blocks, gates, ups):
    rows = sum(b.shape[0] for b in blocks)
    width = gates[0].shape[0]
    return pl.pallas_call(
        functools.partial(gate_up_kernel, len(blocks)),
        out_shape=jax.ShapeDtypeStruct((rows, 3 * LANES), bf16),
        in_specs=[VMEM] * (len(blocks) + 4),
        out_specs=VMEM,
        compiler_params=pltpu.CompilerParams(vmem_limit_bytes=32 << 20),
        cost_estimate=pl.CostEstimate(
            flops=8 * rows * width * LANES, bytes_accessed=8 * width * LANES, transcendentals=0
        ),
    )(*blocks, *gates, *ups)


def down_kernel(count, *refs):
    actives, downs, downs2 = refs[:count], refs[count : 2 * count], refs[2 * count : 3 * count]
    facts_ref, out_ref = refs[3 * count :]
    cols = downs[0].shape[0]
    step = 128
    weights = [
        jnp.concatenate([one[...], two[...]], axis=1) for one, two in zip(downs, downs2)
    ]
    for r in range(0, out_ref.shape[0], step):
        total = 0.0
        for k in range(count):
            total += lax.dot_general(
                actives[k][r : r + step],
                weights[k],
                (((1,), (1,)), ((), ())),
                preferred_element_type=f32,
            )
        facts = facts_ref[r : r + step].astype(f32)
        total *= facts[:, :1] + facts[:, 1:2]
        out_ref[r : r + step, :cols] = total.astype(bf16)
        rest = out_ref.shape[1] - cols
        out_ref[r : r + step, cols:] = jnp.broadcast_to(facts[:, 2:3], (step, rest)).astype(bf16)


def down_sums(actives, downs, downs2, facts):
    rows, cols = actives[0].shape[0], downs[0].shape[0]
    return pl.pallas_call(
        functools.partial(down_kernel, len(actives)),
        out_shape=jax.ShapeDtypeStruct((rows, cols + LANES), bf16),
        in_specs=[VMEM] * (3 * len(actives) + 1),
        out_specs=VMEM,
        compiler_params=pltpu.CompilerParams(vmem_limit_bytes=32 << 20),
    )(*actives, *downs, *downs2, facts)


def ring(block, beside):
    count, cores = lax.axis_size("head"), lax.axis_size("group")
    right = [(i, (i + 1) % count) for i in range(count)]
    left = [(i, (i - 1) % count) for i in range(count)]
    both = [
        (c * count + i, c * count + (i + 1 - 2 * c) % count)
        for c in range(cores)
        for i in range(count)
    ]
    steps, results = [(block,)], []
    for step in range(count // 2):
        held = steps[-1]
        if step < count // 2 - 1:
            got = (lax.ppermute(held[0], "head", right), lax.ppermute(held[-1], "head", left))
        else:
            one = jnp.where(lax.axis_index("group") == 0, held[0], held[-1])
            got = (lax.ppermute(one, ("group", "head"), both),)
        if beside is not None:
            result = beside(held)
            got, result = lax.optimization_barrier((got, result))
            results.append(result)
        steps.append(got)
    if beside is not None:
        results.append(beside(steps[-1]))
    return steps, results


def local(
    queries,
    latent_cache,
    lengths,
    w_value,
    w_out,
    residual,
    norm_gain,
    routes,
    gate_weights,
    w_gate,
    w_up,
    w_down,
):
    reqs = queries.shape[1]
    heads = queries.shape[2]
    latent_width = w_value.shape[1]
    value_width = w_value.shape[2]
    span = latent_cache.shape[2]
    rows = residual.shape[1]
    width = residual.shape[2]
    n_group = lax.axis_size("group")
    n_dp = lax.axis_size("dp")
    n_head = lax.axis_size("head")
    cols = width // n_dp
    piece = width // n_head
    dp = lax.axis_index("dp")
    z = lax.axis_index("head")

    def swap(block):
        return lax.ppermute(block, "group", [(0, 1), (1, 0)])

    gates = (w_gate[0], swap(w_gate[0]))
    ups = (w_up[0], swap(w_up[0]))

    slabs = w_down[0].reshape(n_head, piece, w_down.shape[2])
    downs = []
    for k in range(n_head):
        slab = lax.dynamic_index_in_dim(slabs, lax.rem(z + k, n_head), 0, False)
        if k > 0:
            slab = lax.ppermute(slab, "head", [(i, (i + k) % n_head) for i in range(n_head)])
        downs.append(slab)

    expert_ids = jnp.arange(EXPERTS, dtype=jnp.int32)
    chosen = routes[0][:, :, None] == expert_ids[None, None, :]
    table = jnp.max(jnp.where(chosen, gate_weights[0][:, :, None], -1.0), axis=1)
    table_high = table.astype(bf16)
    table_low = (table - table_high.astype(f32)).astype(bf16)

    cached = latent_cache[0]
    scores = (
        jnp.einsum("rhc,rlc->rhl", queries[0], cached, preferred_element_type=f32) * softmax_scale
    )
    visible = lax.broadcasted_iota(jnp.int32, (reqs, 1, span), 2) < lengths[0][:, None, None]
    scores = jnp.where(visible, scores, -jnp.inf)
    row_max = jnp.max(scores, axis=2, keepdims=True)
    weights = jnp.exp(scores - row_max)
    shares = (weights / jnp.sum(weights, axis=2, keepdims=True)).astype(bf16)
    latent = jnp.einsum(
        "rhl,rlc->rhc", shares, cached[:, :, :latent_width], preferred_element_type=f32
    ).astype(bf16)
    head_rows = jnp.einsum("rhc,hcv->hrv", latent, w_value, preferred_element_type=f32).astype(bf16)

    res = residual[0].reshape(rows, n_dp, cols).transpose(1, 0, 2).reshape(n_dp, -1, value_width)
    res_rows = res.shape[1]
    facts = jnp.stack([table_high.T, table_low.T], axis=1)
    facts = jnp.pad(facts, ((0, 0), (0, -res_rows % 16 - 2), (0, value_width - rows)))
    send = jnp.concatenate(
        [
            jnp.broadcast_to(
                head_rows.reshape(1, heads * reqs, value_width),
                (n_dp, heads * reqs, value_width),
            ),
            res,
            facts,
        ],
        axis=1,
    )
    got = lax.all_to_all(send, "dp", split_axis=0, concat_axis=0, tiled=True)
    got, downs = lax.optimization_barrier((got, downs))
    res_piece = got[:, heads * reqs : heads * reqs + res_rows].reshape(n_dp * rows, cols)
    fact = got[:, heads * reqs + res_rows :, :rows]
    mine = fact[:, 0].reshape(1, n_dp * rows) > 0
    values = got[:, : heads * reqs].reshape(n_dp, heads, n_head, rows, value_width)
    partial = jnp.einsum(
        "dhziv,hvc->zdic",
        values,
        w_out.reshape(heads, value_width, cols),
        preferred_element_type=f32,
    ).astype(bf16)
    partial = lax.all_to_all(
        partial.reshape(n_head, n_dp * rows, cols), "head", split_axis=0, concat_axis=0, tiled=True
    )
    attended = jnp.sum(partial.astype(f32), axis=0).astype(bf16)
    hidden_piece = (res_piece.astype(f32) + attended.astype(f32)).astype(bf16)

    hidden = lax.all_to_all(
        jnp.broadcast_to(hidden_piece[None], (n_dp,) + hidden_piece.shape),
        "dp",
        split_axis=0,
        concat_axis=0,
        tiled=True,
    )
    downs2 = [swap(d) for d in downs]
    hidden, gates, ups, downs2 = lax.optimization_barrier((hidden, gates, ups, downs2))
    home = lax.dynamic_slice(hidden, (0, dp * rows, 0), (n_dp, rows, cols))

    def index(shape, axis):
        return lax.broadcasted_iota(jnp.int32, shape, axis)

    def before(count):
        a, b = index((count, count), 0), index((count, count), 1)
        return ((a // rows == b // rows) & (a < b)).astype(bf16)

    count = n_dp * rows
    slot = jnp.dot(mine.astype(bf16), before(count), preferred_element_type=f32)
    at, of = index((n_dp * CAP, count), 0), index((n_dp * CAP, count), 1)
    pack = (at // CAP == of // rows) & mine & (slot == (at % CAP).astype(f32))
    extra = jnp.concatenate(
        [
            fact[:, :2].transpose(0, 2, 1).reshape(count, 2),
            (index((count, 1), 0) % rows).astype(bf16),
            jnp.zeros((count, LANES - 3), bf16),
        ],
        axis=1,
    )
    packed = norm_pack(hidden, norm_gain.reshape(n_dp, cols), pack.astype(bf16), extra)

    fill = n_dp * CAP
    _, done = ring(packed, lambda blocks: gate_up(blocks, gates, ups))
    active = jnp.concatenate(done, axis=0)

    r = index((1, n_head * fill), 1)
    at = jnp.where(r < fill, 0, (r - fill) // (2 * fill) + 1)
    leftward = (r >= fill) & ((r - fill) // fill % 2 == 1)
    from_z = jnp.where(leftward, z + at, z - at + n_head) % n_head
    to = r % fill // CAP * (n_head * CAP) + from_z * CAP + r % CAP
    order = (index((n_head * fill, n_head * fill), 0) == to).astype(bf16)
    active = jnp.dot(order, active, preferred_element_type=f32).astype(bf16)

    steps, _ = ring(active[:, : 2 * LANES], None)
    actives = [s[0] for s in steps] + [s[1] for s in steps[-2:0:-1]]
    out = down_sums(actives, downs, downs2, active[:, 2 * LANES :])
    out = out.reshape(n_dp, n_head * CAP, -1)
    back = lax.all_to_all(out, "dp", split_axis=0, concat_axis=0, tiled=True)

    back = back.reshape(EXPERTS * n_head * CAP, -1)
    token = (index((back.shape[0], 1), 0) // CAP % n_head * rows).astype(f32)
    token = token + back[:, piece : piece + 1].astype(f32)
    hit = token == index((back.shape[0], n_head * rows), 1).astype(f32)
    mixed = lax.dot_general(
        hit.astype(bf16),
        back[:, :piece],
        (((0,), (0,)), ((), ())),
        preferred_element_type=f32,
    )
    mixed = lax.all_to_all(
        mixed.astype(bf16).reshape(n_head, rows, piece),
        "head",
        split_axis=0,
        concat_axis=0,
        tiled=True,
    )
    home = home.transpose(1, 0, 2).reshape(rows, width)
    mixed = mixed.transpose(1, 0, 2).reshape(rows, width)
    layer_out = (home.astype(f32) + mixed.astype(f32)).astype(bf16)
    return layer_out[None]


def solution(mesh):
    in_specs = (
        P("group", "dp", "head", None),
        P("group", "dp", None, None),
        P("group", "dp"),
        P("head", None, None),
        P("head", "dp"),
        P("group", ("dp", "head"), None),
        P(),
        P("group", ("dp", "head"), None),
        P("group", ("dp", "head"), None),
        P("dp", None, ("group", "head")),
        P("dp", None, ("group", "head")),
        P("dp", None, ("group", "head")),
    )
    out_specs = P("group", ("dp", "head"), None)
    return jax.shard_map(local, mesh=mesh, in_specs=in_specs, out_specs=out_specs, check_vma=False)
```

```python
import functools

import jax
import jax.numpy as jnp
from jax import lax
from jax.experimental import pallas as pl
from jax.experimental.pallas import tpu as pltpu
from jax.sharding import PartitionSpec as P

EXPERTS = 16
CAP = 3


softmax_scale = 0.07216878364870323
norm_eps = 1e-06
bf16 = jnp.bfloat16
f32 = jnp.float32


VMEM = pl.BlockSpec(memory_space=pltpu.VMEM)
SMEM = pl.BlockSpec(memory_space=pltpu.SMEM)
LANES = 128


def attend_kernel(lengths_ref, query_ref, cached_ref, out_ref):
    some, _, width = out_ref.shape
    first = pl.program_id(0) * some
    for r in range(some):
        cached = cached_ref[r]
        scores = (
            lax.dot_general(
                query_ref[r], cached, (((1,), (1,)), ((), ())), preferred_element_type=f32
            )
            * softmax_scale
        )
        visible = lax.broadcasted_iota(jnp.int32, scores.shape, 1) < lengths_ref[first + r]
        scores = jnp.where(visible, scores, -jnp.inf)
        weights = jnp.exp(scores - jnp.max(scores, axis=1, keepdims=True))
        shares = (weights / jnp.sum(weights, axis=1, keepdims=True)).astype(bf16)
        out_ref[r] = jnp.dot(shares, cached[:, :width], preferred_element_type=f32).astype(bf16)


def attend(lengths, queries, cached, width):
    reqs, heads, depth = queries.shape
    some = 4
    return pl.pallas_call(
        attend_kernel,
        out_shape=jax.ShapeDtypeStruct((reqs, heads, width), bf16),
        grid=(reqs // some,),
        in_specs=[
            SMEM,
            pl.BlockSpec((some, heads, depth), lambda i: (i, 0, 0)),
            pl.BlockSpec((some, cached.shape[1], depth), lambda i: (i, 0, 0)),
        ],
        out_specs=pl.BlockSpec((some, heads, width), lambda i: (i, 0, 0)),
        compiler_params=pltpu.CompilerParams(vmem_limit_bytes=32 << 20),
    )(lengths, queries, cached)


def norm_pack_kernel(hidden_ref, gain_ref, pack_ref, extra_ref, out_ref):
    parts, count, cols = hidden_ref.shape
    square = jnp.zeros((count, 1), f32)
    for p in range(parts):
        part = hidden_ref[p].astype(f32)
        square += jnp.sum(part * part, axis=1, keepdims=True)
    scale = lax.rsqrt(square / (parts * cols) + norm_eps)
    pack = pack_ref[...]
    for p in range(parts):
        normed = (hidden_ref[p].astype(f32) * scale * gain_ref[p : p + 1]).astype(bf16)
        rows = jnp.dot(pack, normed, preferred_element_type=f32).astype(bf16)
        out_ref[:, p * cols : (p + 1) * cols] = rows
    extra = jnp.dot(pack, extra_ref[...], preferred_element_type=f32).astype(bf16)
    out_ref[:, parts * cols :] = extra


def norm_pack(hidden, gain, pack, extra):
    parts, _, cols = hidden.shape
    return pl.pallas_call(
        norm_pack_kernel,
        out_shape=jax.ShapeDtypeStruct((pack.shape[0], parts * cols + LANES), bf16),
        in_specs=[VMEM] * 4,
        out_specs=VMEM,
        compiler_params=pltpu.CompilerParams(vmem_limit_bytes=32 << 20),
    )(hidden, gain, pack, extra)


def gate_up_kernel(count, *refs):
    blocks, (gate_ref, gate2_ref, up_ref, up2_ref, out_ref) = refs[:count], refs[count:]
    width = gate_ref.shape[0]
    step = 1024
    gate = up = 0.0
    for k in range(0, width, step):
        rows = jnp.concatenate([b[:, k : k + step] for b in blocks], axis=0)
        weights = jnp.concatenate([gate_ref[k : k + step], gate2_ref[k : k + step]], axis=1)
        gate += jnp.dot(rows, weights, preferred_element_type=f32)
        weights = jnp.concatenate([up_ref[k : k + step], up2_ref[k : k + step]], axis=1)
        up += jnp.dot(rows, weights, preferred_element_type=f32)
    out_ref[:, : 2 * LANES] = (gate / (1.0 + jnp.exp(-gate)) * up).astype(bf16)
    out_ref[:, 2 * LANES :] = jnp.concatenate([b[:, width:] for b in blocks], axis=0)


def gate_up(blocks, gates, ups):
    rows = sum(b.shape[0] for b in blocks)
    width = gates[0].shape[0]
    return pl.pallas_call(
        functools.partial(gate_up_kernel, len(blocks)),
        out_shape=jax.ShapeDtypeStruct((rows, 3 * LANES), bf16),
        in_specs=[VMEM] * (len(blocks) + 4),
        out_specs=VMEM,
        compiler_params=pltpu.CompilerParams(vmem_limit_bytes=32 << 20),
        cost_estimate=pl.CostEstimate(
            flops=8 * rows * width * LANES, bytes_accessed=8 * width * LANES, transcendentals=0
        ),
    )(*blocks, *gates, *ups)


def down_kernel(count, *refs):
    actives, downs, downs2 = refs[:count], refs[count : 2 * count], refs[2 * count : 3 * count]
    facts_ref, out_ref = refs[3 * count :]
    cols = downs[0].shape[0]
    step = 256
    active = jnp.concatenate([a[...] for a in actives], axis=1)
    facts = facts_ref[...].astype(f32)
    weight = facts[:, :1] + facts[:, 1:2]
    for c in range(0, cols, step):
        end = min(c + step, cols)
        weights = [w[c:end] for pair in zip(downs, downs2) for w in pair]
        total = lax.dot_general(
            active,
            jnp.concatenate(weights, axis=1),
            (((1,), (1,)), ((), ())),
            preferred_element_type=f32,
        )
        out_ref[:, c:end] = (total * weight).astype(bf16)
    rest = out_ref.shape[1] - cols
    out_ref[:, cols:] = jnp.broadcast_to(facts[:, 2:3], (facts.shape[0], rest)).astype(bf16)


def down_sums(actives, downs, downs2, facts):
    rows, cols = actives[0].shape[0], downs[0].shape[0]
    return pl.pallas_call(
        functools.partial(down_kernel, len(actives)),
        out_shape=jax.ShapeDtypeStruct((rows, cols + LANES), bf16),
        in_specs=[VMEM] * (3 * len(actives) + 1),
        out_specs=VMEM,
        compiler_params=pltpu.CompilerParams(vmem_limit_bytes=32 << 20),
    )(*actives, *downs, *downs2, facts)


def ring(block, beside):
    count, cores = lax.axis_size("head"), lax.axis_size("group")
    right = [(i, (i + 1) % count) for i in range(count)]
    left = [(i, (i - 1) % count) for i in range(count)]
    both = [
        (c * count + i, c * count + (i + 1 - 2 * c) % count)
        for c in range(cores)
        for i in range(count)
    ]
    steps, results = [(block,)], []
    for step in range(count // 2):
        held = steps[-1]
        if step < count // 2 - 1:
            got = (lax.ppermute(held[0], "head", right), lax.ppermute(held[-1], "head", left))
        else:
            one = jnp.where(lax.axis_index("group") == 0, held[0], held[-1])
            got = (lax.ppermute(one, ("group", "head"), both),)
        if beside is not None:
            result = beside(held)
            got, result = lax.optimization_barrier((got, result))
            results.append(result)
        steps.append(got)
    if beside is not None:
        results.append(beside(steps[-1]))
    return steps, results


def local(
    queries,
    latent_cache,
    lengths,
    w_value,
    w_out,
    residual,
    norm_gain,
    routes,
    gate_weights,
    w_gate,
    w_up,
    w_down,
):
    reqs = queries.shape[1]
    heads = queries.shape[2]
    latent_width = w_value.shape[1]
    value_width = w_value.shape[2]
    rows = residual.shape[1]
    width = residual.shape[2]
    n_group = lax.axis_size("group")
    n_dp = lax.axis_size("dp")
    n_head = lax.axis_size("head")
    cols = width // n_dp
    piece = width // n_head
    dp = lax.axis_index("dp")
    z = lax.axis_index("head")

    def swap(block):
        return lax.ppermute(block, "group", [(0, 1), (1, 0)])

    gates = (w_gate[0], swap(w_gate[0]))
    ups = (w_up[0], swap(w_up[0]))

    right = [(i, (i + 1) % n_head) for i in range(n_head)]
    left = [(i, (i - 1) % n_head) for i in range(n_head)]
    twice = jnp.concatenate([w_down[0], w_down[0]], axis=0)
    slabs = lax.dynamic_slice_in_dim(twice, z * piece, width, 0)
    middle = width // 2 + piece // 2
    downs = [slabs[:piece]] + [None] * (n_head - 1)

    def hop(up, down, k):
        up, down = lax.ppermute(up, "head", right), lax.ppermute(down, "head", left)
        if k == n_head // 2:
            downs[k] = jnp.concatenate([up, down], axis=0)
            return None
        downs[k], downs[n_head - k] = up[:piece], down[-piece:]
        return up[piece:], down[:-piece]

    expert_ids = jnp.arange(EXPERTS, dtype=jnp.int32)
    chosen = routes[0][:, :, None] == expert_ids[None, None, :]
    table = jnp.max(jnp.where(chosen, gate_weights[0][:, :, None], -1.0), axis=1)
    table_high = table.astype(bf16)
    table_low = (table - table_high.astype(f32)).astype(bf16)

    latent = attend(lengths[0], queries[0], latent_cache[0], latent_width)
    head_rows = jnp.einsum("rhc,hcv->hrv", latent, w_value, preferred_element_type=f32).astype(bf16)

    res = residual[0].reshape(rows, n_dp, cols).transpose(1, 0, 2).reshape(n_dp, -1, value_width)
    res_rows = res.shape[1]
    facts = jnp.stack([table_high.T, table_low.T], axis=1)
    facts = jnp.pad(facts, ((0, 0), (0, -res_rows % 16 - 2), (0, value_width - rows)))
    send = jnp.concatenate(
        [
            jnp.broadcast_to(
                head_rows.reshape(1, heads * reqs, value_width),
                (n_dp, heads * reqs, value_width),
            ),
            res,
            facts,
        ],
        axis=1,
    )
    got = lax.all_to_all(send, "dp", split_axis=0, concat_axis=0, tiled=True)
    rest = hop(slabs[piece:middle], slabs[middle:], 1)
    got, rest = lax.optimization_barrier((got, rest))
    res_piece = got[:, heads * reqs : heads * reqs + res_rows].reshape(n_dp * rows, cols)
    fact = got[:, heads * reqs + res_rows :, :rows]
    mine = fact[:, 0].reshape(1, n_dp * rows) > 0
    values = got[:, : heads * reqs].reshape(n_dp, heads, n_head, rows, value_width)
    partial = jnp.einsum(
        "dhziv,hvc->zdic",
        values,
        w_out.reshape(heads, value_width, cols),
        preferred_element_type=f32,
    ).astype(bf16)
    partial = lax.all_to_all(
        partial.reshape(n_head, n_dp * rows, cols), "head", split_axis=0, concat_axis=0, tiled=True
    )
    rest = hop(*rest, 2)
    partial, rest = lax.optimization_barrier((partial, rest))
    attended = jnp.sum(partial.astype(f32), axis=0).astype(bf16)
    hidden_piece = (res_piece.astype(f32) + attended.astype(f32)).astype(bf16)

    hidden = lax.all_to_all(
        jnp.broadcast_to(hidden_piece[None], (n_dp,) + hidden_piece.shape),
        "dp",
        split_axis=0,
        concat_axis=0,
        tiled=True,
    )
    hop(*hop(*rest, 3), 4)
    downs2 = [swap(d) for d in downs]
    hidden, gates, ups, downs2 = lax.optimization_barrier((hidden, gates, ups, downs2))
    home = lax.dynamic_slice(hidden, (0, dp * rows, 0), (n_dp, rows, cols))

    def index(shape, axis):
        return lax.broadcasted_iota(jnp.int32, shape, axis)

    def before(count):
        a, b = index((count, count), 0), index((count, count), 1)
        return ((a // rows == b // rows) & (a < b)).astype(bf16)

    count = n_dp * rows
    slot = jnp.dot(mine.astype(bf16), before(count), preferred_element_type=f32)
    at, of = index((n_dp * CAP, count), 0), index((n_dp * CAP, count), 1)
    pack = (at // CAP == of // rows) & mine & (slot == (at % CAP).astype(f32))
    extra = jnp.concatenate(
        [
            fact[:, :2].transpose(0, 2, 1).reshape(count, 2),
            (index((count, 1), 0) % rows).astype(bf16),
            jnp.zeros((count, LANES - 3), bf16),
        ],
        axis=1,
    )
    packed = norm_pack(hidden, norm_gain.reshape(n_dp, cols), pack.astype(bf16), extra)

    fill = n_dp * CAP
    _, done = ring(packed, lambda blocks: gate_up(blocks, gates, ups))
    active = jnp.concatenate(done, axis=0)

    r = index((1, n_head * fill), 1)
    at = jnp.where(r < fill, 0, (r - fill) // (2 * fill) + 1)
    leftward = (r >= fill) & ((r - fill) // fill % 2 == 1)
    from_z = jnp.where(leftward, z + at, z - at + n_head) % n_head
    to = r % fill // CAP * (n_head * CAP) + from_z * CAP + r % CAP
    order = (index((n_head * fill, n_head * fill), 0) == to).astype(bf16)
    active = jnp.dot(order, active, preferred_element_type=f32).astype(bf16)

    steps, _ = ring(active[:, : 2 * LANES], None)
    actives = [s[0] for s in steps] + [s[1] for s in steps[-2:0:-1]]
    out = down_sums(actives, downs, downs2, active[:, 2 * LANES :])
    out = out.reshape(n_dp, n_head * CAP, -1)
    back = lax.all_to_all(out, "dp", split_axis=0, concat_axis=0, tiled=True)

    back = back.reshape(EXPERTS * n_head * CAP, -1)
    token = (index((back.shape[0], 1), 0) // CAP % n_head * rows).astype(f32)
    token = token + back[:, piece : piece + 1].astype(f32)
    hit = token == index((back.shape[0], n_head * rows), 1).astype(f32)
    mixed = lax.dot_general(
        hit.astype(bf16),
        back[:, :piece],
        (((0,), (0,)), ((), ())),
        preferred_element_type=f32,
    )
    mixed = lax.all_to_all(
        mixed.astype(bf16).reshape(n_head, rows, piece),
        "head",
        split_axis=0,
        concat_axis=0,
        tiled=True,
    )
    home = home.transpose(1, 0, 2).reshape(rows, width)
    mixed = mixed.transpose(1, 0, 2).reshape(rows, width)
    layer_out = (home.astype(f32) + mixed.astype(f32)).astype(bf16)
    return layer_out[None]


def solution(mesh):
    in_specs = (
        P("group", "dp", "head", None),
        P("group", "dp", None, None),
        P("group", "dp"),
        P("head", None, None),
        P("head", "dp"),
        P("group", ("dp", "head"), None),
        P(),
        P("group", ("dp", "head"), None),
        P("group", ("dp", "head"), None),
        P("dp", None, ("group", "head")),
        P("dp", None, ("group", "head")),
        P("dp", None, ("group", "head")),
    )
    out_specs = P("group", ("dp", "head"), None)
    return jax.shard_map(local, mesh=mesh, in_specs=in_specs, out_specs=out_specs, check_vma=False)
```

```python
import functools

import jax
import jax.numpy as jnp
from jax import lax
from jax.experimental import pallas as pl
from jax.experimental.pallas import tpu as pltpu
from jax.sharding import PartitionSpec as P

EXPERTS = 16
CAP = 3


softmax_scale = 0.07216878364870323
norm_eps = 1e-06
bf16 = jnp.bfloat16
f32 = jnp.float32


VMEM = pl.BlockSpec(memory_space=pltpu.VMEM)
SMEM = pl.BlockSpec(memory_space=pltpu.SMEM)
LANES = 128


def norm_pack_kernel(hidden_ref, gain_ref, pack_ref, extra_ref, out_ref):
    parts, count, cols = hidden_ref.shape
    square = jnp.zeros((count, 1), f32)
    for p in range(parts):
        part = hidden_ref[p].astype(f32)
        square += jnp.sum(part * part, axis=1, keepdims=True)
    scale = lax.rsqrt(square / (parts * cols) + norm_eps)
    pack = pack_ref[...]
    for p in range(parts):
        normed = (hidden_ref[p].astype(f32) * scale * gain_ref[p : p + 1]).astype(bf16)
        rows = jnp.dot(pack, normed, preferred_element_type=f32).astype(bf16)
        out_ref[:, p * cols : (p + 1) * cols] = rows
    extra = jnp.dot(pack, extra_ref[...], preferred_element_type=f32).astype(bf16)
    out_ref[:, parts * cols :] = extra


def norm_pack(hidden, gain, pack, extra):
    parts, _, cols = hidden.shape
    return pl.pallas_call(
        norm_pack_kernel,
        out_shape=jax.ShapeDtypeStruct((pack.shape[0], parts * cols + LANES), bf16),
        in_specs=[VMEM] * 4,
        out_specs=VMEM,
        compiler_params=pltpu.CompilerParams(vmem_limit_bytes=32 << 20),
    )(hidden, gain, pack, extra)


def gate_up_kernel(count, *refs):
    blocks, (gate_ref, gate2_ref, up_ref, up2_ref, out_ref) = refs[:count], refs[count:]
    width = gate_ref.shape[0]
    step = 1024
    gate = up = 0.0
    for k in range(0, width, step):
        rows = jnp.concatenate([b[:, k : k + step] for b in blocks], axis=0)
        weights = jnp.concatenate([gate_ref[k : k + step], gate2_ref[k : k + step]], axis=1)
        gate += jnp.dot(rows, weights, preferred_element_type=f32)
        weights = jnp.concatenate([up_ref[k : k + step], up2_ref[k : k + step]], axis=1)
        up += jnp.dot(rows, weights, preferred_element_type=f32)
    out_ref[:, : 2 * LANES] = (gate / (1.0 + jnp.exp(-gate)) * up).astype(bf16)
    out_ref[:, 2 * LANES :] = jnp.concatenate([b[:, width:] for b in blocks], axis=0)


def gate_up(blocks, gates, ups):
    rows = sum(b.shape[0] for b in blocks)
    width = gates[0].shape[0]
    return pl.pallas_call(
        functools.partial(gate_up_kernel, len(blocks)),
        out_shape=jax.ShapeDtypeStruct((rows, 3 * LANES), bf16),
        in_specs=[VMEM] * (len(blocks) + 4),
        out_specs=VMEM,
        compiler_params=pltpu.CompilerParams(vmem_limit_bytes=32 << 20),
        cost_estimate=pl.CostEstimate(
            flops=8 * rows * width * LANES, bytes_accessed=8 * width * LANES, transcendentals=0
        ),
    )(*blocks, *gates, *ups)


def down_kernel(count, *refs):
    actives, downs, downs2 = refs[:count], refs[count : 2 * count], refs[2 * count : 3 * count]
    facts_ref, out_ref = refs[3 * count :]
    cols = downs[0].shape[0]
    step = 256
    active = jnp.concatenate([a[...] for a in actives], axis=1)
    facts = facts_ref[...].astype(f32)
    weight = facts[:, :1] + facts[:, 1:2]
    for c in range(0, cols, step):
        end = min(c + step, cols)
        weights = [w[c:end] for pair in zip(downs, downs2) for w in pair]
        total = lax.dot_general(
            active,
            jnp.concatenate(weights, axis=1),
            (((1,), (1,)), ((), ())),
            preferred_element_type=f32,
        )
        out_ref[:, c:end] = (total * weight).astype(bf16)
    rest = out_ref.shape[1] - cols
    out_ref[:, cols:] = jnp.broadcast_to(facts[:, 2:3], (facts.shape[0], rest)).astype(bf16)


def down_sums(actives, downs, downs2, facts):
    rows, cols = actives[0].shape[0], downs[0].shape[0]
    return pl.pallas_call(
        functools.partial(down_kernel, len(actives)),
        out_shape=jax.ShapeDtypeStruct((rows, cols + LANES), bf16),
        in_specs=[VMEM] * (3 * len(actives) + 1),
        out_specs=VMEM,
        compiler_params=pltpu.CompilerParams(vmem_limit_bytes=32 << 20),
    )(*actives, *downs, *downs2, facts)


def ring(block, beside):
    count, cores = lax.axis_size("head"), lax.axis_size("group")
    right = [(i, (i + 1) % count) for i in range(count)]
    left = [(i, (i - 1) % count) for i in range(count)]
    both = [
        (c * count + i, c * count + (i + 1 - 2 * c) % count)
        for c in range(cores)
        for i in range(count)
    ]
    steps, results = [(block,)], []
    for step in range(count // 2):
        held = steps[-1]
        if step < count // 2 - 1:
            got = (lax.ppermute(held[0], "head", right), lax.ppermute(held[-1], "head", left))
        else:
            one = jnp.where(lax.axis_index("group") == 0, held[0], held[-1])
            got = (lax.ppermute(one, ("group", "head"), both),)
        if beside is not None:
            result = beside(held)
            got, result = lax.optimization_barrier((got, result))
            results.append(result)
        steps.append(got)
    if beside is not None:
        results.append(beside(steps[-1]))
    return steps, results


def local(
    queries,
    latent_cache,
    lengths,
    w_value,
    w_out,
    residual,
    norm_gain,
    routes,
    gate_weights,
    w_gate,
    w_up,
    w_down,
):
    reqs = queries.shape[1]
    heads = queries.shape[2]
    latent_width = w_value.shape[1]
    value_width = w_value.shape[2]
    span = latent_cache.shape[2]
    rows = residual.shape[1]
    width = residual.shape[2]
    n_group = lax.axis_size("group")
    n_dp = lax.axis_size("dp")
    n_head = lax.axis_size("head")
    cols = width // n_dp
    piece = width // n_head
    dp = lax.axis_index("dp")
    z = lax.axis_index("head")

    def swap(block):
        return lax.ppermute(block, "group", [(0, 1), (1, 0)])

    gates = (w_gate[0], swap(w_gate[0]))
    ups = (w_up[0], swap(w_up[0]))

    slabs = w_down[0].reshape(n_head, piece, w_down.shape[2])
    slabs = [
        lax.dynamic_index_in_dim(slabs, lax.rem(z + k, n_head), 0, False) for k in range(n_head)
    ]
    downs = slabs[:1] + [None] * (n_head - 1)

    def shift(k):
        downs[k] = lax.ppermute(slabs[k], "head", [(i, (i + k) % n_head) for i in range(n_head)])

    expert_ids = jnp.arange(EXPERTS, dtype=jnp.int32)
    chosen = routes[0][:, :, None] == expert_ids[None, None, :]
    table = jnp.max(jnp.where(chosen, gate_weights[0][:, :, None], -1.0), axis=1)
    table_high = table.astype(bf16)
    table_low = (table - table_high.astype(f32)).astype(bf16)

    cached = latent_cache[0]
    scores = (
        jnp.einsum("rhc,rlc->rhl", queries[0], cached, preferred_element_type=f32) * softmax_scale
    )
    visible = lax.broadcasted_iota(jnp.int32, (reqs, 1, span), 2) < lengths[0][:, None, None]
    scores = jnp.where(visible, scores, -jnp.inf)
    row_max = jnp.max(scores, axis=2, keepdims=True)
    weights = jnp.exp(scores - row_max)
    shares = (weights / jnp.sum(weights, axis=2, keepdims=True)).astype(bf16)
    latent = jnp.einsum(
        "rhl,rlc->rhc", shares, cached[:, :, :latent_width], preferred_element_type=f32
    ).astype(bf16)
    head_rows = jnp.einsum("rhc,hcv->hrv", latent, w_value, preferred_element_type=f32).astype(bf16)

    res = residual[0].reshape(rows, n_dp, cols).transpose(1, 0, 2).reshape(n_dp, -1, value_width)
    res_rows = res.shape[1]
    facts = jnp.stack([table_high.T, table_low.T], axis=1)
    facts = jnp.pad(facts, ((0, 0), (0, -res_rows % 16 - 2), (0, value_width - rows)))
    send = jnp.concatenate(
        [
            jnp.broadcast_to(
                head_rows.reshape(1, heads * reqs, value_width),
                (n_dp, heads * reqs, value_width),
            ),
            res,
            facts,
        ],
        axis=1,
    )
    got = lax.all_to_all(send, "dp", split_axis=0, concat_axis=0, tiled=True)
    for k in (1, 7, 2, 6):
        shift(k)
    wave = lax.optimization_barrier((downs[1], downs[7], slabs[3], slabs[5], slabs[4]))
    downs[1], downs[7], slabs[3], slabs[5], slabs[4] = wave
    for k in (3, 5, 4):
        shift(k)
    got, downs = lax.optimization_barrier((got, downs))
    res_piece = got[:, heads * reqs : heads * reqs + res_rows].reshape(n_dp * rows, cols)
    fact = got[:, heads * reqs + res_rows :, :rows]
    mine = fact[:, 0].reshape(1, n_dp * rows) > 0
    values = got[:, : heads * reqs].reshape(n_dp, heads, n_head, rows, value_width)
    partial = jnp.einsum(
        "dhziv,hvc->zdic",
        values,
        w_out.reshape(heads, value_width, cols),
        preferred_element_type=f32,
    ).astype(bf16)
    partial = lax.all_to_all(
        partial.reshape(n_head, n_dp * rows, cols), "head", split_axis=0, concat_axis=0, tiled=True
    )
    partial, gates, ups = lax.optimization_barrier((partial, gates, ups))
    attended = jnp.sum(partial.astype(f32), axis=0).astype(bf16)
    hidden_piece = (res_piece.astype(f32) + attended.astype(f32)).astype(bf16)

    hidden = lax.all_to_all(
        jnp.broadcast_to(hidden_piece[None], (n_dp,) + hidden_piece.shape),
        "dp",
        split_axis=0,
        concat_axis=0,
        tiled=True,
    )
    downs2 = [swap(d) for d in downs]
    hidden, downs2 = lax.optimization_barrier((hidden, downs2))
    home = lax.dynamic_slice(hidden, (0, dp * rows, 0), (n_dp, rows, cols))

    def index(shape, axis):
        return lax.broadcasted_iota(jnp.int32, shape, axis)

    def before(count):
        a, b = index((count, count), 0), index((count, count), 1)
        return ((a // rows == b // rows) & (a < b)).astype(bf16)

    count = n_dp * rows
    slot = jnp.dot(mine.astype(bf16), before(count), preferred_element_type=f32)
    at, of = index((n_dp * CAP, count), 0), index((n_dp * CAP, count), 1)
    pack = (at // CAP == of // rows) & mine & (slot == (at % CAP).astype(f32))
    extra = jnp.concatenate(
        [
            fact[:, :2].transpose(0, 2, 1).reshape(count, 2),
            (index((count, 1), 0) % rows).astype(bf16),
            jnp.zeros((count, LANES - 3), bf16),
        ],
        axis=1,
    )
    packed = norm_pack(hidden, norm_gain.reshape(n_dp, cols), pack.astype(bf16), extra)

    fill = n_dp * CAP
    _, done = ring(packed, lambda blocks: gate_up(blocks, gates, ups))
    active = jnp.concatenate(done, axis=0)

    r = index((1, n_head * fill), 1)
    at = jnp.where(r < fill, 0, (r - fill) // (2 * fill) + 1)
    leftward = (r >= fill) & ((r - fill) // fill % 2 == 1)
    from_z = jnp.where(leftward, z + at, z - at + n_head) % n_head
    to = r % fill // CAP * (n_head * CAP) + from_z * CAP + r % CAP
    order = (index((n_head * fill, n_head * fill), 0) == to).astype(bf16)
    active = jnp.dot(order, active, preferred_element_type=f32).astype(bf16)

    steps, _ = ring(active[:, : 2 * LANES], None)
    actives = [s[0] for s in steps] + [s[1] for s in steps[-2:0:-1]]
    out = down_sums(actives, downs, downs2, active[:, 2 * LANES :])
    out = out.reshape(n_dp, n_head * CAP, -1)
    back = lax.all_to_all(out, "dp", split_axis=0, concat_axis=0, tiled=True)

    back = back.reshape(EXPERTS * n_head * CAP, -1)
    token = (index((back.shape[0], 1), 0) // CAP % n_head * rows).astype(f32)
    token = token + back[:, piece : piece + 1].astype(f32)
    hit = token == index((back.shape[0], n_head * rows), 1).astype(f32)
    mixed = lax.dot_general(
        hit.astype(bf16),
        back[:, :piece],
        (((0,), (0,)), ((), ())),
        preferred_element_type=f32,
    )
    mixed = lax.all_to_all(
        mixed.astype(bf16).reshape(n_head, rows, piece),
        "head",
        split_axis=0,
        concat_axis=0,
        tiled=True,
    )
    home = home.transpose(1, 0, 2).reshape(rows, width)
    mixed = mixed.transpose(1, 0, 2).reshape(rows, width)
    layer_out = (home.astype(f32) + mixed.astype(f32)).astype(bf16)
    return layer_out[None]


def solution(mesh):
    in_specs = (
        P("group", "dp", "head", None),
        P("group", "dp", None, None),
        P("group", "dp"),
        P("head", None, None),
        P("head", "dp"),
        P("group", ("dp", "head"), None),
        P(),
        P("group", ("dp", "head"), None),
        P("group", ("dp", "head"), None),
        P("dp", None, ("group", "head")),
        P("dp", None, ("group", "head")),
        P("dp", None, ("group", "head")),
    )
    out_specs = P("group", ("dp", "head"), None)
    return jax.shard_map(local, mesh=mesh, in_specs=in_specs, out_specs=out_specs, check_vma=False)
```

```python
import functools

import jax
import jax.numpy as jnp
from jax import lax
from jax.experimental import pallas as pl
from jax.experimental.pallas import tpu as pltpu
from jax.sharding import PartitionSpec as P

EXPERTS = 16
CAP = 3


softmax_scale = 0.07216878364870323
norm_eps = 1e-06
bf16 = jnp.bfloat16
f32 = jnp.float32


VMEM = pl.BlockSpec(memory_space=pltpu.VMEM)
SMEM = pl.BlockSpec(memory_space=pltpu.SMEM)
LANES = 128


def norm_pack_kernel(hidden_ref, gain_ref, pack_ref, extra_ref, out_ref):
    parts, count, cols = hidden_ref.shape
    square = jnp.zeros((count, 1), f32)
    for p in range(parts):
        part = hidden_ref[p].astype(f32)
        square += jnp.sum(part * part, axis=1, keepdims=True)
    scale = lax.rsqrt(square / (parts * cols) + norm_eps)
    pack = pack_ref[...]
    for p in range(parts):
        normed = (hidden_ref[p].astype(f32) * scale * gain_ref[p : p + 1]).astype(bf16)
        rows = jnp.dot(pack, normed, preferred_element_type=f32).astype(bf16)
        out_ref[:, p * cols : (p + 1) * cols] = rows
    extra = jnp.dot(pack, extra_ref[...], preferred_element_type=f32).astype(bf16)
    out_ref[:, parts * cols :] = extra


def norm_pack(hidden, gain, pack, extra):
    parts, _, cols = hidden.shape
    return pl.pallas_call(
        norm_pack_kernel,
        out_shape=jax.ShapeDtypeStruct((pack.shape[0], parts * cols + LANES), bf16),
        in_specs=[VMEM] * 4,
        out_specs=VMEM,
        compiler_params=pltpu.CompilerParams(vmem_limit_bytes=32 << 20),
    )(hidden, gain, pack, extra)


def merge_kernel(partial_ref, residual_ref, out_ref):
    total = partial_ref[0].astype(f32)
    for k in range(1, partial_ref.shape[0]):
        total += partial_ref[k].astype(f32)
    attended = total.astype(bf16).astype(f32)
    hidden = (residual_ref[...].astype(f32) + attended).astype(bf16)
    for p in range(out_ref.shape[0]):
        out_ref[p] = hidden


def merge(partial, residual, copies):
    return pl.pallas_call(
        merge_kernel,
        out_shape=jax.ShapeDtypeStruct((copies,) + residual.shape, bf16),
        in_specs=[VMEM] * 2,
        out_specs=VMEM,
        compiler_params=pltpu.CompilerParams(vmem_limit_bytes=32 << 20),
    )(partial, residual)


def gate_up_kernel(count, *refs):
    blocks, (gate_ref, gate2_ref, up_ref, up2_ref, out_ref) = refs[:count], refs[count:]
    width = gate_ref.shape[0]
    step = 1024
    gate = up = 0.0
    for k in range(0, width, step):
        rows = jnp.concatenate([b[:, k : k + step] for b in blocks], axis=0)
        weights = jnp.concatenate([gate_ref[k : k + step], gate2_ref[k : k + step]], axis=1)
        gate += jnp.dot(rows, weights, preferred_element_type=f32)
        weights = jnp.concatenate([up_ref[k : k + step], up2_ref[k : k + step]], axis=1)
        up += jnp.dot(rows, weights, preferred_element_type=f32)
    out_ref[:, : 2 * LANES] = (gate / (1.0 + jnp.exp(-gate)) * up).astype(bf16)
    out_ref[:, 2 * LANES :] = jnp.concatenate([b[:, width:] for b in blocks], axis=0)


def gate_up(blocks, gates, ups):
    rows = sum(b.shape[0] for b in blocks)
    width = gates[0].shape[0]
    return pl.pallas_call(
        functools.partial(gate_up_kernel, len(blocks)),
        out_shape=jax.ShapeDtypeStruct((rows, 3 * LANES), bf16),
        in_specs=[VMEM] * (len(blocks) + 4),
        out_specs=VMEM,
        compiler_params=pltpu.CompilerParams(vmem_limit_bytes=32 << 20),
        cost_estimate=pl.CostEstimate(
            flops=8 * rows * width * LANES, bytes_accessed=8 * width * LANES, transcendentals=0
        ),
    )(*blocks, *gates, *ups)


def down_kernel(count, *refs):
    actives, downs, downs2 = refs[:count], refs[count : 2 * count], refs[2 * count : 3 * count]
    facts_ref, out_ref = refs[3 * count :]
    cols = downs[0].shape[0]
    step = 256
    active = jnp.concatenate([a[...] for a in actives], axis=1)
    facts = facts_ref[...].astype(f32)
    weight = facts[:, :1] + facts[:, 1:2]
    for c in range(0, cols, step):
        end = min(c + step, cols)
        weights = [w[c:end] for pair in zip(downs, downs2) for w in pair]
        total = lax.dot_general(
            active,
            jnp.concatenate(weights, axis=1),
            (((1,), (1,)), ((), ())),
            preferred_element_type=f32,
        )
        out_ref[:, c:end] = (total * weight).astype(bf16)
    rest = out_ref.shape[1] - cols
    out_ref[:, cols:] = jnp.broadcast_to(facts[:, 2:3], (facts.shape[0], rest)).astype(bf16)


def down_sums(actives, downs, downs2, facts):
    rows, cols = actives[0].shape[0], downs[0].shape[0]
    return pl.pallas_call(
        functools.partial(down_kernel, len(actives)),
        out_shape=jax.ShapeDtypeStruct((rows, cols + LANES), bf16),
        in_specs=[VMEM] * (3 * len(actives) + 1),
        out_specs=VMEM,
        compiler_params=pltpu.CompilerParams(vmem_limit_bytes=32 << 20),
    )(*actives, *downs, *downs2, facts)


def ring(block, beside):
    count, cores = lax.axis_size("head"), lax.axis_size("group")
    right = [(i, (i + 1) % count) for i in range(count)]
    left = [(i, (i - 1) % count) for i in range(count)]
    both = [
        (c * count + i, c * count + (i + 1 - 2 * c) % count)
        for c in range(cores)
        for i in range(count)
    ]
    steps, results = [(block,)], []
    for step in range(count // 2):
        held = steps[-1]
        if step < count // 2 - 1:
            got = (lax.ppermute(held[0], "head", right), lax.ppermute(held[-1], "head", left))
        else:
            one = jnp.where(lax.axis_index("group") == 0, held[0], held[-1])
            got = (lax.ppermute(one, ("group", "head"), both),)
        if beside is not None:
            result = beside(held)
            got, result = lax.optimization_barrier((got, result))
            results.append(result)
        steps.append(got)
    if beside is not None:
        results.append(beside(steps[-1]))
    return steps, results


def local(
    queries,
    latent_cache,
    lengths,
    w_value,
    w_out,
    residual,
    norm_gain,
    routes,
    gate_weights,
    w_gate,
    w_up,
    w_down,
):
    reqs = queries.shape[1]
    heads = queries.shape[2]
    latent_width = w_value.shape[1]
    value_width = w_value.shape[2]
    span = latent_cache.shape[2]
    rows = residual.shape[1]
    width = residual.shape[2]
    n_group = lax.axis_size("group")
    n_dp = lax.axis_size("dp")
    n_head = lax.axis_size("head")
    cols = width // n_dp
    piece = width // n_head
    dp = lax.axis_index("dp")
    z = lax.axis_index("head")

    def swap(block):
        return lax.ppermute(block, "group", [(0, 1), (1, 0)])

    gates = (w_gate[0], swap(w_gate[0]))
    ups = (w_up[0], swap(w_up[0]))

    slabs = w_down[0].reshape(n_head, piece, w_down.shape[2])
    slabs = [
        lax.dynamic_index_in_dim(slabs, lax.rem(z + k, n_head), 0, False) for k in range(n_head)
    ]
    downs = slabs[:1] + [None] * (n_head - 1)

    def shift(k):
        downs[k] = lax.ppermute(slabs[k], "head", [(i, (i + k) % n_head) for i in range(n_head)])

    expert_ids = jnp.arange(EXPERTS, dtype=jnp.int32)
    chosen = routes[0][:, :, None] == expert_ids[None, None, :]
    table = jnp.max(jnp.where(chosen, gate_weights[0][:, :, None], -1.0), axis=1)
    table_high = table.astype(bf16)
    table_low = (table - table_high.astype(f32)).astype(bf16)

    cached = latent_cache[0]
    scores = (
        jnp.einsum("rhc,rlc->rhl", queries[0], cached, preferred_element_type=f32) * softmax_scale
    )
    visible = lax.broadcasted_iota(jnp.int32, (reqs, 1, span), 2) < lengths[0][:, None, None]
    scores = jnp.where(visible, scores, -jnp.inf)
    row_max = jnp.max(scores, axis=2, keepdims=True)
    weights = jnp.exp(scores - row_max)
    shares = (weights / jnp.sum(weights, axis=2, keepdims=True)).astype(bf16)
    latent = jnp.einsum(
        "rhl,rlc->rhc", shares, cached[:, :, :latent_width], preferred_element_type=f32
    ).astype(bf16)
    head_rows = jnp.einsum("rhc,hcv->hrv", latent, w_value, preferred_element_type=f32).astype(bf16)

    res = residual[0].reshape(rows, n_dp, cols).transpose(1, 0, 2).reshape(n_dp, -1, value_width)
    res_rows = res.shape[1]
    facts = jnp.stack([table_high.T, table_low.T], axis=1)
    facts = jnp.pad(facts, ((0, 0), (0, -res_rows % 16 - 2), (0, value_width - rows)))
    send = jnp.concatenate(
        [
            jnp.broadcast_to(
                head_rows.reshape(1, heads * reqs, value_width),
                (n_dp, heads * reqs, value_width),
            ),
            res,
            facts,
        ],
        axis=1,
    )
    got = lax.all_to_all(send, "dp", split_axis=0, concat_axis=0, tiled=True)
    got, slabs = lax.optimization_barrier((got, slabs))
    for k in (1, 7, 2, 6, 3, 5, 4):
        shift(k)
    res_piece = got[:, heads * reqs : heads * reqs + res_rows].reshape(n_dp * rows, cols)
    fact = got[:, heads * reqs + res_rows :, :rows]
    mine = fact[:, 0].reshape(1, n_dp * rows) > 0
    values = got[:, : heads * reqs].reshape(n_dp, heads, n_head, rows, value_width)
    partial = jnp.einsum(
        "dhziv,hvc->zdic",
        values,
        w_out.reshape(heads, value_width, cols),
        preferred_element_type=f32,
    ).astype(bf16)
    partial = lax.all_to_all(
        partial.reshape(n_head, n_dp * rows, cols), "head", split_axis=0, concat_axis=0, tiled=True
    )
    partial, gates, ups = lax.optimization_barrier((partial, gates, ups))

    hidden = lax.all_to_all(
        merge(partial, res_piece, n_dp), "dp", split_axis=0, concat_axis=0, tiled=True
    )
    hidden, downs[1], downs[7], downs[2], downs[6], downs[3], downs[5], downs[4] = lax.optimization_barrier((hidden, downs[1], downs[7], downs[2], downs[6], downs[3], downs[5], downs[4]))
    downs2 = [None] * n_head
    for k in (0,):
        downs2[k] = swap(downs[k])
    hidden, downs2[0] = lax.optimization_barrier((hidden, downs2[0]))
    home = lax.dynamic_slice(hidden, (0, dp * rows, 0), (n_dp, rows, cols))

    def index(shape, axis):
        return lax.broadcasted_iota(jnp.int32, shape, axis)

    def before(count):
        a, b = index((count, count), 0), index((count, count), 1)
        return ((a // rows == b // rows) & (a < b)).astype(bf16)

    count = n_dp * rows
    slot = jnp.dot(mine.astype(bf16), before(count), preferred_element_type=f32)
    at, of = index((n_dp * CAP, count), 0), index((n_dp * CAP, count), 1)
    pack = (at // CAP == of // rows) & mine & (slot == (at % CAP).astype(f32))
    extra = jnp.concatenate(
        [
            fact[:, :2].transpose(0, 2, 1).reshape(count, 2),
            (index((count, 1), 0) % rows).astype(bf16),
            jnp.zeros((count, LANES - 3), bf16),
        ],
        axis=1,
    )
    packed = norm_pack(hidden, norm_gain.reshape(n_dp, cols), pack.astype(bf16), extra)

    fill = n_dp * CAP
    _, done = ring(packed, lambda blocks: gate_up(blocks, gates, ups))
    active = jnp.concatenate(done, axis=0)

    r = index((1, n_head * fill), 1)
    at = jnp.where(r < fill, 0, (r - fill) // (2 * fill) + 1)
    leftward = (r >= fill) & ((r - fill) // fill % 2 == 1)
    from_z = jnp.where(leftward, z + at, z - at + n_head) % n_head
    to = r % fill // CAP * (n_head * CAP) + from_z * CAP + r % CAP
    order = (index((n_head * fill, n_head * fill), 0) == to).astype(bf16)
    active = jnp.dot(order, active, preferred_element_type=f32).astype(bf16)

    for k in (1, 7, 2, 6, 3, 5, 4):
        downs2[k] = swap(downs[k])
    active, downs2[1], downs2[7], downs2[2], downs2[6], downs2[3], downs2[5], downs2[4] = lax.optimization_barrier((active, downs2[1], downs2[7], downs2[2], downs2[6], downs2[3], downs2[5], downs2[4]))
    steps, _ = ring(active[:, : 2 * LANES], None)
    actives = [s[0] for s in steps] + [s[1] for s in steps[-2:0:-1]]
    out = down_sums(actives, downs, downs2, active[:, 2 * LANES :])
    out = out.reshape(n_dp, n_head * CAP, -1)
    back = lax.all_to_all(out, "dp", split_axis=0, concat_axis=0, tiled=True)

    back = back.reshape(EXPERTS * n_head * CAP, -1)
    token = (index((back.shape[0], 1), 0) // CAP % n_head * rows).astype(f32)
    token = token + back[:, piece : piece + 1].astype(f32)
    hit = token == index((back.shape[0], n_head * rows), 1).astype(f32)
    mixed = lax.dot_general(
        hit.astype(bf16),
        back[:, :piece],
        (((0,), (0,)), ((), ())),
        preferred_element_type=f32,
    )
    mixed = lax.all_to_all(
        mixed.astype(bf16).reshape(n_head, rows, piece),
        "head",
        split_axis=0,
        concat_axis=0,
        tiled=True,
    )
    home = home.transpose(1, 0, 2).reshape(rows, width)
    mixed = mixed.transpose(1, 0, 2).reshape(rows, width)
    layer_out = (home.astype(f32) + mixed.astype(f32)).astype(bf16)
    return layer_out[None]


def solution(mesh):
    in_specs = (
        P("group", "dp", "head", None),
        P("group", "dp", None, None),
        P("group", "dp"),
        P("head", None, None),
        P("head", "dp"),
        P("group", ("dp", "head"), None),
        P(),
        P("group", ("dp", "head"), None),
        P("group", ("dp", "head"), None),
        P("dp", None, ("group", "head")),
        P("dp", None, ("group", "head")),
        P("dp", None, ("group", "head")),
    )
    out_specs = P("group", ("dp", "head"), None)
    return jax.shard_map(local, mesh=mesh, in_specs=in_specs, out_specs=out_specs, check_vma=False)
```

```python
import functools

import jax
import jax.numpy as jnp
from jax import lax
from jax.experimental import pallas as pl
from jax.experimental.pallas import tpu as pltpu
from jax.sharding import PartitionSpec as P

EXPERTS = 16
CAP = 3


softmax_scale = 0.07216878364870323
norm_eps = 1e-06
bf16 = jnp.bfloat16
f32 = jnp.float32


VMEM = pl.BlockSpec(memory_space=pltpu.VMEM)
SMEM = pl.BlockSpec(memory_space=pltpu.SMEM)
LANES = 128


def norm_pack_kernel(hidden_ref, gain_ref, pack_ref, extra_ref, out_ref):
    parts, count, cols = hidden_ref.shape
    kept = cols - LANES
    square = jnp.zeros((count, 1), f32)
    for p in range(parts):
        part = hidden_ref[p].astype(f32)
        square += jnp.sum(part * part, axis=1, keepdims=True)
    scale = lax.rsqrt(square / (parts * cols) + norm_eps)
    pack = pack_ref[...]
    for p in range(parts):
        part = hidden_ref[p, :, :kept].astype(f32)
        normed = (part * scale * gain_ref[p : p + 1, :kept]).astype(bf16)
        rows = jnp.dot(pack, normed, preferred_element_type=f32).astype(bf16)
        out_ref[:, p * kept : (p + 1) * kept] = rows
    high = scale.astype(bf16).astype(f32)
    lane = lax.broadcasted_iota(jnp.int32, extra_ref.shape, 1)
    extra = jnp.where(lane == 3, high, extra_ref[...].astype(f32))
    extra = jnp.where(lane == 4, scale - high, extra).astype(bf16)
    extra = jnp.dot(pack, extra, preferred_element_type=f32).astype(bf16)
    out_ref[:, parts * kept :] = extra


def norm_pack(hidden, gain, pack, extra):
    parts, _, cols = hidden.shape
    return pl.pallas_call(
        norm_pack_kernel,
        out_shape=jax.ShapeDtypeStruct((pack.shape[0], parts * (cols - LANES) + LANES), bf16),
        in_specs=[VMEM] * 4,
        out_specs=VMEM,
        compiler_params=pltpu.CompilerParams(vmem_limit_bytes=32 << 20),
    )(hidden, gain, pack, extra)


def merge_kernel(partial_ref, residual_ref, gain_ref, out_ref, side_ref):
    total = partial_ref[0].astype(f32)
    for k in range(1, partial_ref.shape[0]):
        total += partial_ref[k].astype(f32)
    attended = total.astype(bf16).astype(f32)
    hidden = (residual_ref[...].astype(f32) + attended).astype(bf16)
    for p in range(out_ref.shape[0]):
        out_ref[p] = hidden
    side_ref[...] = (hidden[:, -LANES:].astype(f32) * gain_ref[...]).astype(bf16)


def merge(partial, residual, gain, copies):
    return pl.pallas_call(
        merge_kernel,
        out_shape=(
            jax.ShapeDtypeStruct((copies,) + residual.shape, bf16),
            jax.ShapeDtypeStruct((residual.shape[0], LANES), bf16),
        ),
        in_specs=[VMEM] * 3,
        out_specs=(VMEM, VMEM),
        compiler_params=pltpu.CompilerParams(vmem_limit_bytes=32 << 20),
    )(partial, residual, gain)


def gate_up_kernel(count, *refs):
    blocks, (gate_ref, gate2_ref, up_ref, up2_ref, *outs) = refs[:count], refs[count:]
    width = gate_ref.shape[0]
    step = 1024
    gate = up = 0.0
    for k in range(0, width, step):
        rows = jnp.concatenate([b[:, k : k + step] for b in blocks], axis=0)
        weights = jnp.concatenate([gate_ref[k : k + step], gate2_ref[k : k + step]], axis=1)
        gate += jnp.dot(rows, weights, preferred_element_type=f32)
        weights = jnp.concatenate([up_ref[k : k + step], up2_ref[k : k + step]], axis=1)
        up += jnp.dot(rows, weights, preferred_element_type=f32)
    out_ref, facts_ref = outs
    out_ref[:, : 2 * LANES] = gate
    out_ref[:, 2 * LANES :] = up
    facts_ref[...] = jnp.concatenate([b[:, width:] for b in blocks], axis=0)


def gate_up(blocks, gates, ups):
    rows = sum(b.shape[0] for b in blocks)
    width = gates[0].shape[0]
    return pl.pallas_call(
        functools.partial(gate_up_kernel, len(blocks)),
        out_shape=(
            jax.ShapeDtypeStruct((rows, 4 * LANES), f32),
            jax.ShapeDtypeStruct((rows, LANES), bf16),
        ),
        in_specs=[VMEM] * (len(blocks) + 4),
        out_specs=(VMEM, VMEM),
        compiler_params=pltpu.CompilerParams(vmem_limit_bytes=32 << 20),
        cost_estimate=pl.CostEstimate(
            flops=8 * rows * width * LANES, bytes_accessed=8 * width * LANES, transcendentals=0
        ),
    )(*blocks, *gates, *ups)


def finish_kernel(places, *refs):
    steps = len(places)
    sums, facts, refs = refs[:steps], refs[steps : 2 * steps], refs[2 * steps :]
    side_ref, gate_ref, gate2_ref, up_ref, up2_ref, out_ref, dense = refs
    parts, tokens, _ = side_ref.shape
    weights = jnp.concatenate([w[...] for w in (gate_ref, gate2_ref, up_ref, up2_ref)], axis=1)
    step = 256
    for t in range(0, tokens, step):
        rows = jnp.concatenate([side_ref[p, t : t + step] for p in range(parts)], axis=1)
        dense[t : t + step] = jnp.dot(rows, weights, preferred_element_type=f32)
    count = tokens // sum(len(p) for p in places)
    fill = out_ref.shape[0] // sum(len(p) for p in places)
    at = 0
    for some, sum_ref, fact_ref in zip(places, sums, facts):
        for b, place in enumerate(some):
            fact = fact_ref[b * fill : (b + 1) * fill]
            fact_f = fact.astype(f32)
            token = lax.broadcasted_iota(jnp.int32, (fill, count), 1).astype(f32)
            hit = (token == fact_f[:, 5:6]).astype(f32).astype(bf16)
            picked = dense[place * count : (place + 1) * count]
            high = picked.astype(bf16)
            low = (picked - high.astype(f32)).astype(bf16)
            picked = jnp.dot(hit, high, preferred_element_type=f32) + jnp.dot(
                hit, low, preferred_element_type=f32
            )
            total = sum_ref[b * fill : (b + 1) * fill] + picked * (fact_f[:, 3:4] + fact_f[:, 4:5])
            gate, up = total[:, : 2 * LANES], total[:, 2 * LANES :]
            active = (gate / (1.0 + jnp.exp(-gate)) * up).astype(bf16)
            out_ref[at : at + fill, : 2 * LANES] = active
            out_ref[at : at + fill, 2 * LANES :] = fact
            at += fill


def finish(places, done, side, weights):
    rows = sum(d[0].shape[0] for d in done)
    return pl.pallas_call(
        functools.partial(finish_kernel, places),
        out_shape=jax.ShapeDtypeStruct((rows, 3 * LANES), bf16),
        in_specs=[VMEM] * (2 * len(done) + 5),
        out_specs=VMEM,
        scratch_shapes=[pltpu.VMEM((side.shape[1], 4 * LANES), f32)],
        compiler_params=pltpu.CompilerParams(vmem_limit_bytes=32 << 20),
    )(*[d[0] for d in done], *[d[1] for d in done], side, *weights)


def by_distance(steps):
    return [s[0] for s in steps] + [s[1] for s in steps[-2:0:-1]]


def down_kernel(count, *refs):
    actives, downs, downs2 = refs[:count], refs[count : 2 * count], refs[2 * count : 3 * count]
    facts_ref, out_ref = refs[3 * count :]
    cols = downs[0].shape[0]
    step = 256
    active = jnp.concatenate([a[...] for a in actives], axis=1)
    facts = facts_ref[...].astype(f32)
    weight = facts[:, :1] + facts[:, 1:2]
    for c in range(0, cols, step):
        end = min(c + step, cols)
        weights = [w[c:end] for pair in zip(downs, downs2) for w in pair]
        total = lax.dot_general(
            active,
            jnp.concatenate(weights, axis=1),
            (((1,), (1,)), ((), ())),
            preferred_element_type=f32,
        )
        out_ref[:, c:end] = (total * weight).astype(bf16)
    rest = out_ref.shape[1] - cols
    out_ref[:, cols:] = jnp.broadcast_to(facts[:, 2:3], (facts.shape[0], rest)).astype(bf16)


def down_sums(actives, downs, downs2, facts):
    rows, cols = actives[0].shape[0], downs[0].shape[0]
    return pl.pallas_call(
        functools.partial(down_kernel, len(actives)),
        out_shape=jax.ShapeDtypeStruct((rows, cols + LANES), bf16),
        in_specs=[VMEM] * (3 * len(actives) + 1),
        out_specs=VMEM,
        compiler_params=pltpu.CompilerParams(vmem_limit_bytes=32 << 20),
    )(*actives, *downs, *downs2, facts)


def ring(block, beside):
    count, cores = lax.axis_size("head"), lax.axis_size("group")
    right = [(i, (i + 1) % count) for i in range(count)]
    left = [(i, (i - 1) % count) for i in range(count)]
    both = [
        (c * count + i, c * count + (i + 1 - 2 * c) % count)
        for c in range(cores)
        for i in range(count)
    ]
    steps, results = [(block,)], []
    for step in range(count // 2):
        held = steps[-1]
        if step < count // 2 - 1:
            got = (lax.ppermute(held[0], "head", right), lax.ppermute(held[-1], "head", left))
        else:
            one = jnp.where(lax.axis_index("group") == 0, held[0], held[-1])
            got = (lax.ppermute(one, ("group", "head"), both),)
        if beside is not None:
            result = beside(step, held)
            got, result = lax.optimization_barrier((got, result))
            results.append(result)
        steps.append(got)
    if beside is not None:
        results.append(beside(count // 2, steps[-1]))
    return steps, results


def local(
    queries,
    latent_cache,
    lengths,
    w_value,
    w_out,
    residual,
    norm_gain,
    routes,
    gate_weights,
    w_gate,
    w_up,
    w_down,
):
    reqs = queries.shape[1]
    heads = queries.shape[2]
    latent_width = w_value.shape[1]
    value_width = w_value.shape[2]
    span = latent_cache.shape[2]
    rows = residual.shape[1]
    width = residual.shape[2]
    n_group = lax.axis_size("group")
    n_dp = lax.axis_size("dp")
    n_head = lax.axis_size("head")
    cols = width // n_dp
    piece = width // n_head
    dp = lax.axis_index("dp")
    z = lax.axis_index("head")

    def swap(block):
        return lax.ppermute(block, "group", [(0, 1), (1, 0)])

    def both(weight):
        weight = weight.reshape(n_dp, cols, weight.shape[1])
        main = weight[:, :-LANES].reshape(-1, weight.shape[2])
        side = weight[:, -LANES:].reshape(-1, weight.shape[2])
        return (main, swap(main)), (side, swap(side))

    slabs = w_down[0].reshape(n_head, piece, w_down.shape[2])
    slabs = [
        lax.dynamic_index_in_dim(slabs, lax.rem(z + k, n_head), 0, False) for k in range(n_head)
    ]
    downs = slabs[:1] + [None] * (n_head - 1)

    def shift(k):
        downs[k] = lax.ppermute(slabs[k], "head", [(i, (i + k) % n_head) for i in range(n_head)])

    expert_ids = jnp.arange(EXPERTS, dtype=jnp.int32)
    chosen = routes[0][:, :, None] == expert_ids[None, None, :]
    table = jnp.max(jnp.where(chosen, gate_weights[0][:, :, None], -1.0), axis=1)
    table_high = table.astype(bf16)
    table_low = (table - table_high.astype(f32)).astype(bf16)

    cached = latent_cache[0]
    scores = (
        jnp.einsum("rhc,rlc->rhl", queries[0], cached, preferred_element_type=f32) * softmax_scale
    )
    visible = lax.broadcasted_iota(jnp.int32, (reqs, 1, span), 2) < lengths[0][:, None, None]
    scores = jnp.where(visible, scores, -jnp.inf)
    row_max = jnp.max(scores, axis=2, keepdims=True)
    weights = jnp.exp(scores - row_max)
    shares = (weights / jnp.sum(weights, axis=2, keepdims=True)).astype(bf16)
    latent = jnp.einsum(
        "rhl,rlc->rhc", shares, cached[:, :, :latent_width], preferred_element_type=f32
    ).astype(bf16)
    head_rows = jnp.einsum("rhc,hcv->hrv", latent, w_value, preferred_element_type=f32).astype(bf16)

    res = residual[0].reshape(rows, n_dp, cols).transpose(1, 0, 2).reshape(n_dp, -1, value_width)
    res_rows = res.shape[1]
    facts = jnp.stack([table_high.T, table_low.T], axis=1)
    facts = jnp.pad(facts, ((0, 0), (0, -res_rows % 16 - 2), (0, value_width - rows)))
    send = jnp.concatenate(
        [
            jnp.broadcast_to(
                head_rows.reshape(1, heads * reqs, value_width),
                (n_dp, heads * reqs, value_width),
            ),
            res,
            facts,
        ],
        axis=1,
    )
    got = lax.all_to_all(send, "dp", split_axis=0, concat_axis=0, tiled=True)
    got, slabs, gate_w, up_w = lax.optimization_barrier((got, slabs, w_gate[0], w_up[0]))
    gates, side_gates = both(gate_w)
    ups, side_ups = both(up_w)
    for k in (1, 7, 2, 6, 3, 5, 4):
        shift(k)
    res_piece = got[:, heads * reqs : heads * reqs + res_rows].reshape(n_dp * rows, cols)
    fact = got[:, heads * reqs + res_rows :, :rows]
    mine = fact[:, 0].reshape(1, n_dp * rows) > 0
    values = got[:, : heads * reqs].reshape(n_dp, heads, n_head, rows, value_width)
    partial = jnp.einsum(
        "dhziv,hvc->zdic",
        values,
        w_out.reshape(heads, value_width, cols),
        preferred_element_type=f32,
    ).astype(bf16)
    partial = lax.all_to_all(
        partial.reshape(n_head, n_dp * rows, cols), "head", split_axis=0, concat_axis=0, tiled=True
    )
    beside = lax.optimization_barrier((partial, gates, ups, side_gates, side_ups))
    partial, gates, ups, side_gates, side_ups = beside

    side_gain = lax.dynamic_slice(norm_gain.reshape(n_dp, cols), (dp, cols - LANES), (1, LANES))
    copies, side = merge(partial, res_piece, side_gain, n_dp)
    hidden = lax.all_to_all(copies, "dp", split_axis=0, concat_axis=0, tiled=True)
    side = jnp.concatenate(by_distance(ring(side, None)[0]), axis=0)
    hidden, side = lax.optimization_barrier((hidden, side))
    hidden, downs[1], downs[7], downs[2], downs[6], downs[3], downs[5], downs[4] = lax.optimization_barrier((hidden, downs[1], downs[7], downs[2], downs[6], downs[3], downs[5], downs[4]))
    downs2 = [None] * n_head
    for k in (0,):
        downs2[k] = swap(downs[k])
    hidden, downs2[0] = lax.optimization_barrier((hidden, downs2[0]))
    home = lax.dynamic_slice(hidden, (0, dp * rows, 0), (n_dp, rows, cols))

    def index(shape, axis):
        return lax.broadcasted_iota(jnp.int32, shape, axis)

    def before(count):
        a, b = index((count, count), 0), index((count, count), 1)
        return ((a // rows == b // rows) & (a < b)).astype(bf16)

    count = n_dp * rows
    slot = jnp.dot(mine.astype(bf16), before(count), preferred_element_type=f32)
    at, of = index((n_dp * CAP, count), 0), index((n_dp * CAP, count), 1)
    pack = (at // CAP == of // rows) & mine & (slot == (at % CAP).astype(f32))
    extra = jnp.concatenate(
        [
            fact[:, :2].transpose(0, 2, 1).reshape(count, 2),
            (index((count, 1), 0) % rows).astype(bf16),
            jnp.zeros((count, 2), bf16),
            index((count, 1), 0).astype(bf16),
            jnp.zeros((count, LANES - 6), bf16),
        ],
        axis=1,
    )
    packed = norm_pack(hidden, norm_gain.reshape(n_dp, cols), pack.astype(bf16), extra)

    fill = n_dp * CAP
    side = lax.all_to_all(
        jnp.broadcast_to(side[None], (n_dp,) + side.shape),
        "dp",
        split_axis=0,
        concat_axis=0,
        tiled=True,
    )
    half = n_head // 2
    work = lambda step, blocks: (gate_up(blocks, gates, ups), side if step == half - 2 else None)
    _, done = ring(packed, work)
    side = done[half - 2][1]
    done = [d[0] for d in done]
    places = [(0,)] + [(k, n_head - k) for k in range(1, half)] + [(half,)]
    active = finish(places, done, side, side_gates + side_ups)

    r = index((1, n_head * fill), 1)
    at = jnp.where(r < fill, 0, (r - fill) // (2 * fill) + 1)
    leftward = (r >= fill) & ((r - fill) // fill % 2 == 1)
    from_z = jnp.where(leftward, z + at, z - at + n_head) % n_head
    to = r % fill // CAP * (n_head * CAP) + from_z * CAP + r % CAP
    order = (index((n_head * fill, n_head * fill), 0) == to).astype(bf16)
    active = jnp.dot(order, active, preferred_element_type=f32).astype(bf16)

    for k in (1, 7, 2, 6, 3, 5, 4):
        downs2[k] = swap(downs[k])
    active, downs2[1], downs2[7], downs2[2], downs2[6], downs2[3], downs2[5], downs2[4] = lax.optimization_barrier((active, downs2[1], downs2[7], downs2[2], downs2[6], downs2[3], downs2[5], downs2[4]))
    steps, _ = ring(active[:, : 2 * LANES], None)
    actives = by_distance(steps)
    out = down_sums(actives, downs, downs2, active[:, 2 * LANES :])
    out = out.reshape(n_dp, n_head * CAP, -1)
    back = lax.all_to_all(out, "dp", split_axis=0, concat_axis=0, tiled=True)

    back = back.reshape(EXPERTS * n_head * CAP, -1)
    token = (index((back.shape[0], 1), 0) // CAP % n_head * rows).astype(f32)
    token = token + back[:, piece : piece + 1].astype(f32)
    hit = token == index((back.shape[0], n_head * rows), 1).astype(f32)
    mixed = lax.dot_general(
        hit.astype(bf16),
        back[:, :piece],
        (((0,), (0,)), ((), ())),
        preferred_element_type=f32,
    )
    mixed = lax.all_to_all(
        mixed.astype(bf16).reshape(n_head, rows, piece),
        "head",
        split_axis=0,
        concat_axis=0,
        tiled=True,
    )
    home = home.transpose(1, 0, 2).reshape(rows, width)
    mixed = mixed.transpose(1, 0, 2).reshape(rows, width)
    layer_out = (home.astype(f32) + mixed.astype(f32)).astype(bf16)
    return layer_out[None]


def solution(mesh):
    in_specs = (
        P("group", "dp", "head", None),
        P("group", "dp", None, None),
        P("group", "dp"),
        P("head", None, None),
        P("head", "dp"),
        P("group", ("dp", "head"), None),
        P(),
        P("group", ("dp", "head"), None),
        P("group", ("dp", "head"), None),
        P("dp", None, ("group", "head")),
        P("dp", None, ("group", "head")),
        P("dp", None, ("group", "head")),
    )
    out_specs = P("group", ("dp", "head"), None)
    return jax.shard_map(local, mesh=mesh, in_specs=in_specs, out_specs=out_specs, check_vma=False)
```

```python
import functools

import jax
import jax.numpy as jnp
from jax import lax
from jax.experimental import pallas as pl
from jax.experimental.pallas import tpu as pltpu
from jax.sharding import PartitionSpec as P

EXPERTS = 16
CAP = 3


softmax_scale = 0.07216878364870323
norm_eps = 1e-06
bf16 = jnp.bfloat16
f32 = jnp.float32


VMEM = pl.BlockSpec(memory_space=pltpu.VMEM)
SMEM = pl.BlockSpec(memory_space=pltpu.SMEM)
LANES = 128


def norm_pack_kernel(hidden_ref, gain_ref, pack_ref, extra_ref, out_ref):
    parts, count, cols = hidden_ref.shape
    kept = cols - LANES
    square = jnp.zeros((count, 1), f32)
    for p in range(parts):
        part = hidden_ref[p].astype(f32)
        square += jnp.sum(part * part, axis=1, keepdims=True)
    scale = lax.rsqrt(square / (parts * cols) + norm_eps)
    pack = pack_ref[...]
    for p in range(parts):
        part = hidden_ref[p, :, :kept].astype(f32)
        normed = (part * scale * gain_ref[p : p + 1, :kept]).astype(bf16)
        rows = jnp.dot(pack, normed, preferred_element_type=f32).astype(bf16)
        out_ref[:, p * kept : (p + 1) * kept] = rows
    high = scale.astype(bf16).astype(f32)
    lane = lax.broadcasted_iota(jnp.int32, extra_ref.shape, 1)
    extra = jnp.where(lane == 3, high, extra_ref[...].astype(f32))
    extra = jnp.where(lane == 4, scale - high, extra).astype(bf16)
    extra = jnp.dot(pack, extra, preferred_element_type=f32).astype(bf16)
    out_ref[:, parts * kept :] = extra


def norm_pack(hidden, gain, pack, extra):
    parts, _, cols = hidden.shape
    return pl.pallas_call(
        norm_pack_kernel,
        out_shape=jax.ShapeDtypeStruct((pack.shape[0], parts * (cols - LANES) + LANES), bf16),
        in_specs=[VMEM] * 4,
        out_specs=VMEM,
        compiler_params=pltpu.CompilerParams(vmem_limit_bytes=32 << 20),
    )(hidden, gain, pack, extra)


def merge_kernel(partial_ref, residual_ref, gain_ref, out_ref, side_ref):
    total = partial_ref[0].astype(f32)
    for k in range(1, partial_ref.shape[0]):
        total += partial_ref[k].astype(f32)
    attended = total.astype(bf16).astype(f32)
    hidden = (residual_ref[...].astype(f32) + attended).astype(bf16)
    for p in range(out_ref.shape[0]):
        out_ref[p] = hidden
    side_ref[...] = (hidden[:, -LANES:].astype(f32) * gain_ref[...]).astype(bf16)


def merge(partial, residual, gain, copies):
    return pl.pallas_call(
        merge_kernel,
        out_shape=(
            jax.ShapeDtypeStruct((copies,) + residual.shape, bf16),
            jax.ShapeDtypeStruct((residual.shape[0], LANES), bf16),
        ),
        in_specs=[VMEM] * 3,
        out_specs=(VMEM, VMEM),
        compiler_params=pltpu.CompilerParams(vmem_limit_bytes=32 << 20),
    )(partial, residual, gain)


def gate_up_kernel(count, *refs):
    blocks, (gate_ref, gate2_ref, up_ref, up2_ref, *outs) = refs[:count], refs[count:]
    width = gate_ref.shape[0]
    step = 1024
    gate = up = 0.0
    for k in range(0, width, step):
        rows = jnp.concatenate([b[:, k : k + step] for b in blocks], axis=0)
        weights = jnp.concatenate([gate_ref[k : k + step], gate2_ref[k : k + step]], axis=1)
        gate += jnp.dot(rows, weights, preferred_element_type=f32)
        weights = jnp.concatenate([up_ref[k : k + step], up2_ref[k : k + step]], axis=1)
        up += jnp.dot(rows, weights, preferred_element_type=f32)
    out_ref, facts_ref = outs
    out_ref[:, : 2 * LANES] = gate
    out_ref[:, 2 * LANES :] = up
    facts_ref[...] = jnp.concatenate([b[:, width:] for b in blocks], axis=0)


def gate_up(blocks, gates, ups):
    rows = sum(b.shape[0] for b in blocks)
    width = gates[0].shape[0]
    return pl.pallas_call(
        functools.partial(gate_up_kernel, len(blocks)),
        out_shape=(
            jax.ShapeDtypeStruct((rows, 4 * LANES), f32),
            jax.ShapeDtypeStruct((rows, LANES), bf16),
        ),
        in_specs=[VMEM] * (len(blocks) + 4),
        out_specs=(VMEM, VMEM),
        compiler_params=pltpu.CompilerParams(vmem_limit_bytes=32 << 20),
        cost_estimate=pl.CostEstimate(
            flops=8 * rows * width * LANES, bytes_accessed=8 * width * LANES, transcendentals=0
        ),
    )(*blocks, *gates, *ups)


def finish_kernel(places, z_ref, *refs):
    steps = len(places)
    z = z_ref[0]
    n_head = sum(len(p) for p in places)
    sums, facts, refs = refs[:steps], refs[steps : 2 * steps], refs[2 * steps :]
    side_ref, gate_ref, gate2_ref, up_ref, up2_ref, out_ref, dense = refs
    parts, tokens, _ = side_ref.shape
    weights = jnp.concatenate([w[...] for w in (gate_ref, gate2_ref, up_ref, up2_ref)], axis=1)
    step = 256
    for t in range(0, tokens, step):
        rows = jnp.concatenate([side_ref[p, t : t + step] for p in range(parts)], axis=1)
        dense[t : t + step] = jnp.dot(rows, weights, preferred_element_type=f32)
    count = tokens // n_head
    fill = out_ref.shape[0] // n_head
    at = 0
    for some, sum_ref, fact_ref in zip(places, sums, facts):
        for b, place in enumerate(some):
            fact = fact_ref[b * fill : (b + 1) * fill]
            fact_f = fact.astype(f32)
            token = lax.broadcasted_iota(jnp.int32, (fill, count), 1).astype(f32)
            hit = (token == fact_f[:, 5:6]).astype(f32).astype(bf16)
            start = lax.rem(z - place + n_head, n_head) * count
            picked = dense[pl.ds(pl.multiple_of(start, count), count), :]
            high = picked.astype(bf16)
            low = (picked - high.astype(f32)).astype(bf16)
            picked = jnp.dot(hit, high, preferred_element_type=f32) + jnp.dot(
                hit, low, preferred_element_type=f32
            )
            total = sum_ref[b * fill : (b + 1) * fill] + picked * (fact_f[:, 3:4] + fact_f[:, 4:5])
            gate, up = total[:, : 2 * LANES], total[:, 2 * LANES :]
            active = (gate / (1.0 + jnp.exp(-gate)) * up).astype(bf16)
            out_ref[at : at + fill, : 2 * LANES] = active
            out_ref[at : at + fill, 2 * LANES :] = fact
            at += fill


def finish(places, z, done, side, weights):
    rows = sum(d[0].shape[0] for d in done)
    return pl.pallas_call(
        functools.partial(finish_kernel, places),
        out_shape=jax.ShapeDtypeStruct((rows, 3 * LANES), bf16),
        in_specs=[SMEM] + [VMEM] * (2 * len(done) + 5),
        out_specs=VMEM,
        scratch_shapes=[pltpu.VMEM((side.shape[1], 4 * LANES), f32)],
        compiler_params=pltpu.CompilerParams(vmem_limit_bytes=32 << 20),
    )(z.reshape(1), *[d[0] for d in done], *[d[1] for d in done], side, *weights)


def by_distance(steps):
    return [s[0] for s in steps] + [s[1] for s in steps[-2:0:-1]]


def down_kernel(count, *refs):
    actives, downs, downs2 = refs[:count], refs[count : 2 * count], refs[2 * count : 3 * count]
    facts_ref, out_ref = refs[3 * count :]
    cols = downs[0].shape[0]
    step = 256
    active = jnp.concatenate([a[...] for a in actives], axis=1)
    facts = facts_ref[...].astype(f32)
    weight = facts[:, :1] + facts[:, 1:2]
    for c in range(0, cols, step):
        end = min(c + step, cols)
        weights = [w[c:end] for pair in zip(downs, downs2) for w in pair]
        total = lax.dot_general(
            active,
            jnp.concatenate(weights, axis=1),
            (((1,), (1,)), ((), ())),
            preferred_element_type=f32,
        )
        out_ref[:, c:end] = (total * weight).astype(bf16)
    rest = out_ref.shape[1] - cols
    out_ref[:, cols:] = jnp.broadcast_to(facts[:, 2:3], (facts.shape[0], rest)).astype(bf16)


def down_sums(actives, downs, downs2, facts):
    rows, cols = actives[0].shape[0], downs[0].shape[0]
    return pl.pallas_call(
        functools.partial(down_kernel, len(actives)),
        out_shape=jax.ShapeDtypeStruct((rows, cols + LANES), bf16),
        in_specs=[VMEM] * (3 * len(actives) + 1),
        out_specs=VMEM,
        compiler_params=pltpu.CompilerParams(vmem_limit_bytes=32 << 20),
    )(*actives, *downs, *downs2, facts)


def ring(block, beside):
    count, cores = lax.axis_size("head"), lax.axis_size("group")
    right = [(i, (i + 1) % count) for i in range(count)]
    left = [(i, (i - 1) % count) for i in range(count)]
    both = [
        (c * count + i, c * count + (i + 1 - 2 * c) % count)
        for c in range(cores)
        for i in range(count)
    ]
    steps, results = [(block,)], []
    for step in range(count // 2):
        held = steps[-1]
        if step < count // 2 - 1:
            got = (lax.ppermute(held[0], "head", right), lax.ppermute(held[-1], "head", left))
        else:
            one = jnp.where(lax.axis_index("group") == 0, held[0], held[-1])
            got = (lax.ppermute(one, ("group", "head"), both),)
        if beside is not None:
            result = beside(step, held)
            got, result = lax.optimization_barrier((got, result))
            results.append(result)
        steps.append(got)
    if beside is not None:
        results.append(beside(count // 2, steps[-1]))
    return steps, results


def local(
    queries,
    latent_cache,
    lengths,
    w_value,
    w_out,
    residual,
    norm_gain,
    routes,
    gate_weights,
    w_gate,
    w_up,
    w_down,
):
    reqs = queries.shape[1]
    heads = queries.shape[2]
    latent_width = w_value.shape[1]
    value_width = w_value.shape[2]
    span = latent_cache.shape[2]
    rows = residual.shape[1]
    width = residual.shape[2]
    n_group = lax.axis_size("group")
    n_dp = lax.axis_size("dp")
    n_head = lax.axis_size("head")
    cols = width // n_dp
    piece = width // n_head
    dp = lax.axis_index("dp")
    z = lax.axis_index("head")

    def swap(block):
        return lax.ppermute(block, "group", [(0, 1), (1, 0)])

    def both(weight):
        weight = weight.reshape(n_dp, cols, weight.shape[1])
        main = weight[:, :-LANES].reshape(-1, weight.shape[2])
        side = weight[:, -LANES:].reshape(-1, weight.shape[2])
        return (main, swap(main)), (side, swap(side))

    slabs = w_down[0].reshape(n_head, piece, w_down.shape[2])
    slabs = [
        lax.dynamic_index_in_dim(slabs, lax.rem(z + k, n_head), 0, False) for k in range(n_head)
    ]
    downs = slabs[:1] + [None] * (n_head - 1)

    def shift(k):
        downs[k] = lax.ppermute(slabs[k], "head", [(i, (i + k) % n_head) for i in range(n_head)])

    expert_ids = jnp.arange(EXPERTS, dtype=jnp.int32)
    chosen = routes[0][:, :, None] == expert_ids[None, None, :]
    table = jnp.max(jnp.where(chosen, gate_weights[0][:, :, None], -1.0), axis=1)
    table_high = table.astype(bf16)
    table_low = (table - table_high.astype(f32)).astype(bf16)

    cached = latent_cache[0]
    scores = (
        jnp.einsum("rhc,rlc->rhl", queries[0], cached, preferred_element_type=f32) * softmax_scale
    )
    visible = lax.broadcasted_iota(jnp.int32, (reqs, 1, span), 2) < lengths[0][:, None, None]
    scores = jnp.where(visible, scores, -jnp.inf)
    row_max = jnp.max(scores, axis=2, keepdims=True)
    weights = jnp.exp(scores - row_max)
    shares = (weights / jnp.sum(weights, axis=2, keepdims=True)).astype(bf16)
    latent = jnp.einsum(
        "rhl,rlc->rhc", shares, cached[:, :, :latent_width], preferred_element_type=f32
    ).astype(bf16)
    head_rows = jnp.einsum("rhc,hcv->hrv", latent, w_value, preferred_element_type=f32).astype(bf16)

    res = residual[0].reshape(rows, n_dp, cols).transpose(1, 0, 2).reshape(n_dp, -1, value_width)
    res_rows = res.shape[1]
    facts = jnp.stack([table_high.T, table_low.T], axis=1)
    facts = jnp.pad(facts, ((0, 0), (0, -res_rows % 16 - 2), (0, value_width - rows)))
    send = jnp.concatenate(
        [
            jnp.broadcast_to(
                head_rows.reshape(1, heads * reqs, value_width),
                (n_dp, heads * reqs, value_width),
            ),
            res,
            facts,
        ],
        axis=1,
    )
    got = lax.all_to_all(send, "dp", split_axis=0, concat_axis=0, tiled=True)
    got, slabs, gate_w, up_w = lax.optimization_barrier((got, slabs, w_gate[0], w_up[0]))
    gates, side_gates = both(gate_w)
    ups, side_ups = both(up_w)
    for k in (1, 7, 2, 6, 3, 5, 4):
        shift(k)
    res_piece = got[:, heads * reqs : heads * reqs + res_rows].reshape(n_dp * rows, cols)
    fact = got[:, heads * reqs + res_rows :, :rows]
    mine = fact[:, 0].reshape(1, n_dp * rows) > 0
    values = got[:, : heads * reqs].reshape(n_dp, heads, n_head, rows, value_width)
    partial = jnp.einsum(
        "dhziv,hvc->zdic",
        values,
        w_out.reshape(heads, value_width, cols),
        preferred_element_type=f32,
    ).astype(bf16)
    partial = lax.all_to_all(
        partial.reshape(n_head, n_dp * rows, cols), "head", split_axis=0, concat_axis=0, tiled=True
    )
    beside = lax.optimization_barrier((partial, gates, ups, side_gates, side_ups))
    partial, gates, ups, side_gates, side_ups = beside

    side_gain = lax.dynamic_slice(norm_gain.reshape(n_dp, cols), (dp, cols - LANES), (1, LANES))
    copies, side = merge(partial, res_piece, side_gain, n_dp)
    hidden = lax.all_to_all(copies, "dp", split_axis=0, concat_axis=0, tiled=True)
    side = lax.all_to_all(
        jnp.broadcast_to(side[None], (n_head,) + side.shape),
        "head",
        split_axis=0,
        concat_axis=0,
        tiled=True,
    ).reshape(-1, LANES)
    hidden, side = lax.optimization_barrier((hidden, side))
    hidden, downs[1], downs[7], downs[2], downs[6], downs[3], downs[5], downs[4] = lax.optimization_barrier((hidden, downs[1], downs[7], downs[2], downs[6], downs[3], downs[5], downs[4]))
    downs2 = [None] * n_head
    for k in (0,):
        downs2[k] = swap(downs[k])
    hidden, downs2[0] = lax.optimization_barrier((hidden, downs2[0]))
    home = lax.dynamic_slice(hidden, (0, dp * rows, 0), (n_dp, rows, cols))

    def index(shape, axis):
        return lax.broadcasted_iota(jnp.int32, shape, axis)

    def before(count):
        a, b = index((count, count), 0), index((count, count), 1)
        return ((a // rows == b // rows) & (a < b)).astype(bf16)

    count = n_dp * rows
    slot = jnp.dot(mine.astype(bf16), before(count), preferred_element_type=f32)
    at, of = index((n_dp * CAP, count), 0), index((n_dp * CAP, count), 1)
    pack = (at // CAP == of // rows) & mine & (slot == (at % CAP).astype(f32))
    extra = jnp.concatenate(
        [
            fact[:, :2].transpose(0, 2, 1).reshape(count, 2),
            (index((count, 1), 0) % rows).astype(bf16),
            jnp.zeros((count, 2), bf16),
            index((count, 1), 0).astype(bf16),
            jnp.zeros((count, LANES - 6), bf16),
        ],
        axis=1,
    )
    packed = norm_pack(hidden, norm_gain.reshape(n_dp, cols), pack.astype(bf16), extra)

    fill = n_dp * CAP
    side = lax.all_to_all(
        jnp.broadcast_to(side[None], (n_dp,) + side.shape),
        "dp",
        split_axis=0,
        concat_axis=0,
        tiled=True,
    )
    half = n_head // 2
    work = lambda step, blocks: (gate_up(blocks, gates, ups), side if step == half - 2 else None)
    _, done = ring(packed, work)
    side = done[half - 2][1]
    done = [d[0] for d in done]
    places = [(0,)] + [(k, n_head - k) for k in range(1, half)] + [(half,)]
    active = finish(places, z, done, side, side_gates + side_ups)

    r = index((1, n_head * fill), 1)
    at = jnp.where(r < fill, 0, (r - fill) // (2 * fill) + 1)
    leftward = (r >= fill) & ((r - fill) // fill % 2 == 1)
    from_z = jnp.where(leftward, z + at, z - at + n_head) % n_head
    to = r % fill // CAP * (n_head * CAP) + from_z * CAP + r % CAP
    order = (index((n_head * fill, n_head * fill), 0) == to).astype(bf16)
    active = jnp.dot(order, active, preferred_element_type=f32).astype(bf16)

    for k in (1, 7, 2, 6, 3, 5, 4):
        downs2[k] = swap(downs[k])
    active, downs2[1], downs2[7], downs2[2], downs2[6], downs2[3], downs2[5], downs2[4] = lax.optimization_barrier((active, downs2[1], downs2[7], downs2[2], downs2[6], downs2[3], downs2[5], downs2[4]))
    steps, _ = ring(active[:, : 2 * LANES], None)
    actives = by_distance(steps)
    out = down_sums(actives, downs, downs2, active[:, 2 * LANES :])
    out = out.reshape(n_dp, n_head * CAP, -1)
    back = lax.all_to_all(out, "dp", split_axis=0, concat_axis=0, tiled=True)

    back = back.reshape(EXPERTS * n_head * CAP, -1)
    token = (index((back.shape[0], 1), 0) // CAP % n_head * rows).astype(f32)
    token = token + back[:, piece : piece + 1].astype(f32)
    hit = token == index((back.shape[0], n_head * rows), 1).astype(f32)
    mixed = lax.dot_general(
        hit.astype(bf16),
        back[:, :piece],
        (((0,), (0,)), ((), ())),
        preferred_element_type=f32,
    )
    mixed = lax.all_to_all(
        mixed.astype(bf16).reshape(n_head, rows, piece),
        "head",
        split_axis=0,
        concat_axis=0,
        tiled=True,
    )
    home = home.transpose(1, 0, 2).reshape(rows, width)
    mixed = mixed.transpose(1, 0, 2).reshape(rows, width)
    layer_out = (home.astype(f32) + mixed.astype(f32)).astype(bf16)
    return layer_out[None]


def solution(mesh):
    in_specs = (
        P("group", "dp", "head", None),
        P("group", "dp", None, None),
        P("group", "dp"),
        P("head", None, None),
        P("head", "dp"),
        P("group", ("dp", "head"), None),
        P(),
        P("group", ("dp", "head"), None),
        P("group", ("dp", "head"), None),
        P("dp", None, ("group", "head")),
        P("dp", None, ("group", "head")),
        P("dp", None, ("group", "head")),
    )
    out_specs = P("group", ("dp", "head"), None)
    return jax.shard_map(local, mesh=mesh, in_specs=in_specs, out_specs=out_specs, check_vma=False)
```

```python
import functools

import jax
import jax.numpy as jnp
from jax import lax
from jax.experimental import pallas as pl
from jax.experimental.pallas import tpu as pltpu
from jax.sharding import PartitionSpec as P

EXPERTS = 16
CAP = 3


softmax_scale = 0.07216878364870323
norm_eps = 1e-06
bf16 = jnp.bfloat16
f32 = jnp.float32


VMEM = pl.BlockSpec(memory_space=pltpu.VMEM)
SMEM = pl.BlockSpec(memory_space=pltpu.SMEM)
LANES = 128


def norm_pack_kernel(hidden_ref, gain_ref, pack_ref, extra_ref, out_ref):
    parts, count, cols = hidden_ref.shape
    kept = cols - LANES
    square = jnp.zeros((count, 1), f32)
    for p in range(parts):
        part = hidden_ref[p].astype(f32)
        square += jnp.sum(part * part, axis=1, keepdims=True)
    scale = lax.rsqrt(square / (parts * cols) + norm_eps)
    pack = pack_ref[...]
    for p in range(parts):
        part = hidden_ref[p, :, :kept].astype(f32)
        normed = (part * scale * gain_ref[p : p + 1, :kept]).astype(bf16)
        rows = jnp.dot(pack, normed, preferred_element_type=f32).astype(bf16)
        out_ref[:, p * kept : (p + 1) * kept] = rows
    high = scale.astype(bf16).astype(f32)
    lane = lax.broadcasted_iota(jnp.int32, extra_ref.shape, 1)
    extra = jnp.where(lane == 3, high, extra_ref[...].astype(f32))
    extra = jnp.where(lane == 4, scale - high, extra).astype(bf16)
    extra = jnp.dot(pack, extra, preferred_element_type=f32).astype(bf16)
    out_ref[:, parts * kept :] = extra


def norm_pack(hidden, gain, pack, extra):
    parts, _, cols = hidden.shape
    return pl.pallas_call(
        norm_pack_kernel,
        out_shape=jax.ShapeDtypeStruct((pack.shape[0], parts * (cols - LANES) + LANES), bf16),
        in_specs=[VMEM] * 4,
        out_specs=VMEM,
        compiler_params=pltpu.CompilerParams(vmem_limit_bytes=32 << 20),
    )(hidden, gain, pack, extra)


def merge_kernel(partial_ref, residual_ref, gain_ref, out_ref, side_ref):
    total = partial_ref[0].astype(f32)
    for k in range(1, partial_ref.shape[0]):
        total += partial_ref[k].astype(f32)
    attended = total.astype(bf16).astype(f32)
    hidden = (residual_ref[...].astype(f32) + attended).astype(bf16)
    for p in range(out_ref.shape[0]):
        out_ref[p] = hidden
    side_ref[...] = (hidden[:, -LANES:].astype(f32) * gain_ref[...]).astype(bf16)


def merge(partial, residual, gain, copies):
    return pl.pallas_call(
        merge_kernel,
        out_shape=(
            jax.ShapeDtypeStruct((copies,) + residual.shape, bf16),
            jax.ShapeDtypeStruct((residual.shape[0], LANES), bf16),
        ),
        in_specs=[VMEM] * 3,
        out_specs=(VMEM, VMEM),
        compiler_params=pltpu.CompilerParams(vmem_limit_bytes=32 << 20),
    )(partial, residual, gain)


def gate_up_kernel(count, *refs):
    blocks, (gate_ref, gate2_ref, up_ref, up2_ref, *outs) = refs[:count], refs[count:]
    width = gate_ref.shape[0]
    step = 1024
    gate = up = 0.0
    for k in range(0, width, step):
        rows = jnp.concatenate([b[:, k : k + step] for b in blocks], axis=0)
        weights = jnp.concatenate([gate_ref[k : k + step], gate2_ref[k : k + step]], axis=1)
        gate += jnp.dot(rows, weights, preferred_element_type=f32)
        weights = jnp.concatenate([up_ref[k : k + step], up2_ref[k : k + step]], axis=1)
        up += jnp.dot(rows, weights, preferred_element_type=f32)
    out_ref, facts_ref = outs
    out_ref[:, : 2 * LANES] = gate
    out_ref[:, 2 * LANES :] = up
    facts_ref[...] = jnp.concatenate([b[:, width:] for b in blocks], axis=0)


def gate_up(blocks, gates, ups):
    rows = sum(b.shape[0] for b in blocks)
    width = gates[0].shape[0]
    return pl.pallas_call(
        functools.partial(gate_up_kernel, len(blocks)),
        out_shape=(
            jax.ShapeDtypeStruct((rows, 4 * LANES), f32),
            jax.ShapeDtypeStruct((rows, LANES), bf16),
        ),
        in_specs=[VMEM] * (len(blocks) + 4),
        out_specs=(VMEM, VMEM),
        compiler_params=pltpu.CompilerParams(vmem_limit_bytes=32 << 20),
        cost_estimate=pl.CostEstimate(
            flops=8 * rows * width * LANES, bytes_accessed=8 * width * LANES, transcendentals=0
        ),
    )(*blocks, *gates, *ups)


def finish_kernel(places, z_ref, *refs):
    steps = len(places)
    z = z_ref[0]
    n_head = sum(len(p) for p in places)
    sums, facts, refs = refs[:steps], refs[steps : 2 * steps], refs[2 * steps :]
    side_ref, gate_ref, gate2_ref, up_ref, up2_ref, out_ref, dense = refs
    parts, tokens, _ = side_ref.shape
    weights = jnp.concatenate([w[...] for w in (gate_ref, gate2_ref, up_ref, up2_ref)], axis=1)
    step = 256
    for t in range(0, tokens, step):
        rows = jnp.concatenate([side_ref[p, t : t + step] for p in range(parts)], axis=1)
        dense[t : t + step] = jnp.dot(rows, weights, preferred_element_type=f32)
    count = tokens // n_head
    fill = out_ref.shape[0] // n_head
    at = 0
    for some, sum_ref, fact_ref in zip(places, sums, facts):
        for b, place in enumerate(some):
            fact = fact_ref[b * fill : (b + 1) * fill]
            fact_f = fact.astype(f32)
            token = lax.broadcasted_iota(jnp.int32, (fill, count), 1).astype(f32)
            hit = (token == fact_f[:, 5:6]).astype(f32).astype(bf16)
            start = lax.rem(z - place + n_head, n_head) * count
            picked = dense[pl.ds(pl.multiple_of(start, count), count), :]
            high = picked.astype(bf16)
            low = (picked - high.astype(f32)).astype(bf16)
            picked = jnp.dot(hit, high, preferred_element_type=f32) + jnp.dot(
                hit, low, preferred_element_type=f32
            )
            total = sum_ref[b * fill : (b + 1) * fill] + picked * (fact_f[:, 3:4] + fact_f[:, 4:5])
            gate, up = total[:, : 2 * LANES], total[:, 2 * LANES :]
            active = (gate / (1.0 + jnp.exp(-gate)) * up).astype(bf16)
            out_ref[at : at + fill, : 2 * LANES] = active
            out_ref[at : at + fill, 2 * LANES :] = fact
            at += fill


def finish(places, z, done, side, weights):
    rows = sum(d[0].shape[0] for d in done)
    return pl.pallas_call(
        functools.partial(finish_kernel, places),
        out_shape=jax.ShapeDtypeStruct((rows, 3 * LANES), bf16),
        in_specs=[SMEM] + [VMEM] * (2 * len(done) + 5),
        out_specs=VMEM,
        scratch_shapes=[pltpu.VMEM((side.shape[1], 4 * LANES), f32)],
        compiler_params=pltpu.CompilerParams(vmem_limit_bytes=32 << 20),
    )(z.reshape(1), *[d[0] for d in done], *[d[1] for d in done], side, *weights)


def by_distance(steps):
    return [s[0] for s in steps] + [s[1] for s in steps[-2:0:-1]]


def down_kernel(count, *refs):
    actives, downs, downs2 = refs[:count], refs[count : 2 * count], refs[2 * count : 3 * count]
    facts_ref, out_ref = refs[3 * count :]
    cols = downs[0].shape[0]
    step = 256
    active = jnp.concatenate([a[...] for a in actives], axis=1)
    facts = facts_ref[...].astype(f32)
    weight = facts[:, :1] + facts[:, 1:2]
    for c in range(0, cols, step):
        end = min(c + step, cols)
        weights = [w[c:end] for pair in zip(downs, downs2) for w in pair]
        total = lax.dot_general(
            active,
            jnp.concatenate(weights, axis=1),
            (((1,), (1,)), ((), ())),
            preferred_element_type=f32,
        )
        out_ref[:, c:end] = (total * weight).astype(bf16)
    rest = out_ref.shape[1] - cols
    out_ref[:, cols:] = jnp.broadcast_to(facts[:, 2:3], (facts.shape[0], rest)).astype(bf16)


def down_sums(actives, downs, downs2, facts):
    rows, cols = actives[0].shape[0], downs[0].shape[0]
    return pl.pallas_call(
        functools.partial(down_kernel, len(actives)),
        out_shape=jax.ShapeDtypeStruct((rows, cols + LANES), bf16),
        in_specs=[VMEM] * (3 * len(actives) + 1),
        out_specs=VMEM,
        compiler_params=pltpu.CompilerParams(vmem_limit_bytes=32 << 20),
    )(*actives, *downs, *downs2, facts)


def ring(block, beside):
    count, cores = lax.axis_size("head"), lax.axis_size("group")
    right = [(i, (i + 1) % count) for i in range(count)]
    left = [(i, (i - 1) % count) for i in range(count)]
    both = [
        (c * count + i, c * count + (i + 1 - 2 * c) % count)
        for c in range(cores)
        for i in range(count)
    ]
    steps, results = [(block,)], []
    for step in range(count // 2):
        held = steps[-1]
        if step < count // 2 - 1:
            got = (lax.ppermute(held[0], "head", right), lax.ppermute(held[-1], "head", left))
        else:
            one = jnp.where(lax.axis_index("group") == 0, held[0], held[-1])
            got = (lax.ppermute(one, ("group", "head"), both),)
        if beside is not None:
            result = beside(step, held)
            got, result = lax.optimization_barrier((got, result))
            results.append(result)
        steps.append(got)
    if beside is not None:
        results.append(beside(count // 2, steps[-1]))
    return steps, results


def local(
    queries,
    latent_cache,
    lengths,
    w_value,
    w_out,
    residual,
    norm_gain,
    routes,
    gate_weights,
    w_gate,
    w_up,
    w_down,
):
    reqs = queries.shape[1]
    heads = queries.shape[2]
    latent_width = w_value.shape[1]
    value_width = w_value.shape[2]
    span = latent_cache.shape[2]
    rows = residual.shape[1]
    width = residual.shape[2]
    n_group = lax.axis_size("group")
    n_dp = lax.axis_size("dp")
    n_head = lax.axis_size("head")
    cols = width // n_dp
    piece = width // n_head
    dp = lax.axis_index("dp")
    z = lax.axis_index("head")

    def swap(block):
        return lax.ppermute(block, "group", [(0, 1), (1, 0)])

    def both(weight):
        weight = weight.reshape(n_dp, cols, weight.shape[1])
        main = weight[:, :-LANES].reshape(-1, weight.shape[2])
        side = weight[:, -LANES:].reshape(-1, weight.shape[2])
        return (main, swap(main)), (side, swap(side))

    slabs = w_down[0].reshape(n_head, piece, w_down.shape[2])
    slabs = [
        lax.dynamic_index_in_dim(slabs, lax.rem(z + k, n_head), 0, False) for k in range(n_head)
    ]
    downs = slabs[:1] + [None] * (n_head - 1)

    def shift(k):
        downs[k] = lax.ppermute(slabs[k], "head", [(i, (i + k) % n_head) for i in range(n_head)])

    expert_ids = jnp.arange(EXPERTS, dtype=jnp.int32)
    chosen = routes[0][:, :, None] == expert_ids[None, None, :]
    table = jnp.max(jnp.where(chosen, gate_weights[0][:, :, None], -1.0), axis=1)
    table_high = table.astype(bf16)
    table_low = (table - table_high.astype(f32)).astype(bf16)

    cached = latent_cache[0]
    scores = (
        jnp.einsum("rhc,rlc->rhl", queries[0], cached, preferred_element_type=f32) * softmax_scale
    )
    visible = lax.broadcasted_iota(jnp.int32, (reqs, 1, span), 2) < lengths[0][:, None, None]
    scores = jnp.where(visible, scores, -jnp.inf)
    row_max = jnp.max(scores, axis=2, keepdims=True)
    weights = jnp.exp(scores - row_max)
    shares = (weights / jnp.sum(weights, axis=2, keepdims=True)).astype(bf16)
    latent = jnp.einsum(
        "rhl,rlc->rhc", shares, cached[:, :, :latent_width], preferred_element_type=f32
    ).astype(bf16)
    head_rows = jnp.einsum("rhc,hcv->hrv", latent, w_value, preferred_element_type=f32).astype(bf16)

    res = residual[0].reshape(rows, n_dp, cols).transpose(1, 0, 2).reshape(n_dp, -1, value_width)
    res_rows = res.shape[1]
    facts = jnp.stack([table_high.T, table_low.T], axis=1)
    facts = jnp.pad(facts, ((0, 0), (0, -res_rows % 16 - 2), (0, value_width - rows)))
    send = jnp.concatenate(
        [
            jnp.broadcast_to(
                head_rows.reshape(1, heads * reqs, value_width),
                (n_dp, heads * reqs, value_width),
            ),
            res,
            facts,
        ],
        axis=1,
    )
    got = lax.all_to_all(send, "dp", split_axis=0, concat_axis=0, tiled=True)
    gates, side_gates = both(w_gate[0])
    ups, side_ups = both(w_up[0])
    beside = lax.optimization_barrier((got, slabs, gates, ups, side_gates, side_ups))
    got, slabs, gates, ups, side_gates, side_ups = beside
    for k in (1, 7, 2, 6, 3, 5, 4):
        shift(k)
    res_piece = got[:, heads * reqs : heads * reqs + res_rows].reshape(n_dp * rows, cols)
    fact = got[:, heads * reqs + res_rows :, :rows]
    mine = fact[:, 0].reshape(1, n_dp * rows) > 0
    values = got[:, : heads * reqs].reshape(n_dp, heads, n_head, rows, value_width)
    partial = jnp.einsum(
        "dhziv,hvc->zdic",
        values,
        w_out.reshape(heads, value_width, cols),
        preferred_element_type=f32,
    ).astype(bf16)
    partial = lax.all_to_all(
        partial.reshape(n_head, n_dp * rows, cols), "head", split_axis=0, concat_axis=0, tiled=True
    )

    partial, downs[1], downs[7] = lax.optimization_barrier((partial, downs[1], downs[7]))

    side_gain = lax.dynamic_slice(norm_gain.reshape(n_dp, cols), (dp, cols - LANES), (1, LANES))
    copies, side = merge(partial, res_piece, side_gain, n_dp)
    hidden = lax.all_to_all(copies, "dp", split_axis=0, concat_axis=0, tiled=True)
    side = lax.all_to_all(
        jnp.broadcast_to(side[None], (n_head,) + side.shape),
        "head",
        split_axis=0,
        concat_axis=0,
        tiled=True,
    ).reshape(-1, LANES)
    side, downs[2], downs[6] = lax.optimization_barrier((side, downs[2], downs[6]))
    hidden, side = lax.optimization_barrier((hidden, side))
    hidden, downs[1], downs[7], downs[2], downs[6], downs[3], downs[5], downs[4] = lax.optimization_barrier((hidden, downs[1], downs[7], downs[2], downs[6], downs[3], downs[5], downs[4]))
    downs2 = [None] * n_head
    for k in (0,):
        downs2[k] = swap(downs[k])
    hidden, downs2[0] = lax.optimization_barrier((hidden, downs2[0]))
    home = lax.dynamic_slice(hidden, (0, dp * rows, 0), (n_dp, rows, cols))

    def index(shape, axis):
        return lax.broadcasted_iota(jnp.int32, shape, axis)

    def before(count):
        a, b = index((count, count), 0), index((count, count), 1)
        return ((a // rows == b // rows) & (a < b)).astype(bf16)

    count = n_dp * rows
    slot = jnp.dot(mine.astype(bf16), before(count), preferred_element_type=f32)
    at, of = index((n_dp * CAP, count), 0), index((n_dp * CAP, count), 1)
    pack = (at // CAP == of // rows) & mine & (slot == (at % CAP).astype(f32))
    extra = jnp.concatenate(
        [
            fact[:, :2].transpose(0, 2, 1).reshape(count, 2),
            (index((count, 1), 0) % rows).astype(bf16),
            jnp.zeros((count, 2), bf16),
            index((count, 1), 0).astype(bf16),
            jnp.zeros((count, LANES - 6), bf16),
        ],
        axis=1,
    )
    packed = norm_pack(hidden, norm_gain.reshape(n_dp, cols), pack.astype(bf16), extra)

    fill = n_dp * CAP
    side = lax.all_to_all(
        jnp.broadcast_to(side[None], (n_dp,) + side.shape),
        "dp",
        split_axis=0,
        concat_axis=0,
        tiled=True,
    )
    half = n_head // 2
    work = lambda step, blocks: (gate_up(blocks, gates, ups), side if step == half - 2 else None)
    _, done = ring(packed, work)
    side = done[half - 2][1]
    done = [d[0] for d in done]
    places = [(0,)] + [(k, n_head - k) for k in range(1, half)] + [(half,)]
    active = finish(places, z, done, side, side_gates + side_ups)

    r = index((1, n_head * fill), 1)
    at = jnp.where(r < fill, 0, (r - fill) // (2 * fill) + 1)
    leftward = (r >= fill) & ((r - fill) // fill % 2 == 1)
    from_z = jnp.where(leftward, z + at, z - at + n_head) % n_head
    to = r % fill // CAP * (n_head * CAP) + from_z * CAP + r % CAP
    order = (index((n_head * fill, n_head * fill), 0) == to).astype(bf16)
    active = jnp.dot(order, active, preferred_element_type=f32).astype(bf16)

    for k in (1, 7, 2, 6, 3, 5, 4):
        downs2[k] = swap(downs[k])
    active, downs2[1], downs2[7], downs2[2], downs2[6], downs2[3], downs2[5], downs2[4] = lax.optimization_barrier((active, downs2[1], downs2[7], downs2[2], downs2[6], downs2[3], downs2[5], downs2[4]))
    steps, _ = ring(active[:, : 2 * LANES], None)
    actives = by_distance(steps)
    out = down_sums(actives, downs, downs2, active[:, 2 * LANES :])
    out = out.reshape(n_dp, n_head * CAP, -1)
    back = lax.all_to_all(out, "dp", split_axis=0, concat_axis=0, tiled=True)

    back = back.reshape(EXPERTS * n_head * CAP, -1)
    token = (index((back.shape[0], 1), 0) // CAP % n_head * rows).astype(f32)
    token = token + back[:, piece : piece + 1].astype(f32)
    hit = token == index((back.shape[0], n_head * rows), 1).astype(f32)
    mixed = lax.dot_general(
        hit.astype(bf16),
        back[:, :piece],
        (((0,), (0,)), ((), ())),
        preferred_element_type=f32,
    )
    mixed = lax.all_to_all(
        mixed.astype(bf16).reshape(n_head, rows, piece),
        "head",
        split_axis=0,
        concat_axis=0,
        tiled=True,
    )
    home = home.transpose(1, 0, 2).reshape(rows, width)
    mixed = mixed.transpose(1, 0, 2).reshape(rows, width)
    layer_out = (home.astype(f32) + mixed.astype(f32)).astype(bf16)
    return layer_out[None]


def solution(mesh):
    in_specs = (
        P("group", "dp", "head", None),
        P("group", "dp", None, None),
        P("group", "dp"),
        P("head", None, None),
        P("head", "dp"),
        P("group", ("dp", "head"), None),
        P(),
        P("group", ("dp", "head"), None),
        P("group", ("dp", "head"), None),
        P("dp", None, ("group", "head")),
        P("dp", None, ("group", "head")),
        P("dp", None, ("group", "head")),
    )
    out_specs = P("group", ("dp", "head"), None)
    return jax.shard_map(local, mesh=mesh, in_specs=in_specs, out_specs=out_specs, check_vma=False)
```
